32 devices in a mesh: dp: 8 (over y, x, core), tensor: 4 (over z).
Axes of the slice: x: 2, y: 2, z: 4, core: 2. Of those that a mesh axis runs over, the one named last changes fastest.
Arguments:
- patches: float32 [16384, 1152], P(('dp', 'tensor')), may hold values from -16 to 16
- conditioning: float32 [64, 1152], P(('dp', 'tensor')), may hold values from -10 to 10
- time_bins: int32 [64], P(('dp', 'tensor')), may hold values from 0 to 511
- lengths: int32 [64], P(('dp', 'tensor')), may hold values from 32 to 256, as said below
- positions: int32 [2, 16384], P(None, ('dp', 'tensor')), may hold values from 0 to 127, as said below
- time_table: float32 [512, 1152], replicated, may hold values from -3 to 3
- w_ada: bfloat16 [1152, 6912], replicated, may hold values from -0.1875 to 0.1875
- b_ada: float32 [6912], replicated, may hold values from -3 to 3
- w_qkv: bfloat16 [1152, 3, 1152], P(None, None, 'tensor'), may hold values from -0.1875 to 0.1875
- w_out: bfloat16 [1152, 1152], P('tensor'), may hold values from -0.75 to 0.75
- branch_bias: float32 [2304], replicated, may hold values from -2 to 2
- w_gu: bfloat16 [1152, 2, 3072], P(None, None, 'tensor'), may hold values from -0.1875 to 0.1875
- w_down: bfloat16 [3072, 1152], P('tensor'), may hold values from -0.109375 to 0.109375
- d_out: float32 [16384, 1152], P(('dp', 'tensor')), may hold values from -6 to 6
Outputs:
- output: float32 [16384, 1152], P(('dp', 'tensor'))
- d_patches: float32 [16384, 1152], P(('dp', 'tensor'))
- d_conditioning: float32 [64, 1152], P(('dp', 'tensor'))
- d_w_qkv: float32 [1152, 3, 1152], P('dp', None, 'tensor')
- d_w_out: float32 [1152, 1152], P('tensor', 'dp')
- d_w_gu: float32 [1152, 2, 3072], P('dp', None, 'tensor')
- d_w_down: float32 [3072, 1152], P('tensor', 'dp')
- d_w_ada: float32 [1152, 6912], P(None, ('dp', 'tensor'))
- d_b_ada: float32 [6912], P(('dp', 'tensor'))
- d_branch_bias: float32 [2304], P(('dp', 'tensor'))
- d_time_table: float32 [512, 1152], P(('dp', 'tensor'))
- rms: float32 [3], replicated
The draws below stay inside these ranges and needn't reach their ends.
Inputs may be any that keep to these rules, and one draw needn't show every extreme that they name: `lengths`: among the images of each index of dp one, drawn, has exactly 256 valid tokens. `positions`: token i of an image whose grid is w patches wide sits at row i // w and column i % w; w is drawn per image, and the first image's grid is 2 wide.
All inputs are finite; a program needn't handle non-finite values.
Results may differ from the reference program's by a relative error of at most 0.025.
The reference program's roundings to bfloat16 on the way count: a program that leaves them out, or rounds other values in their place, can miss the bound.
Values may be sent and summed in bfloat16 or wider, within the bound.
No kernel may reach another device: no remote copies, remote signals or barrier semaphores. Data moves between devices by JAX's collectives and lax.ppermute only.
A program may use at most 256 MiB of HBM per device.

```python
import math
import jax
import jax.numpy as jnp
from jax import lax

D = 1152
H = 16
HD = 72
FF = 3072
SEQ = 256
BINS = 512
IMG_DEV = 2
IMAGES = 64
TOKENS = 16384
N_TENSOR = 4


def image_growth(count, each, top_factor):
    image_index = (jnp.arange(count, dtype=jnp.int32) // each).astype(jnp.float32)
    return 1.0 + (top_factor - 1.0) * image_index / max(IMAGES - 1, 1)


def draw_patches(key, part):
    key = jax.random.fold_in(key, 11)
    noise = jnp.clip(jax.random.normal(key, (TOKENS, D), jnp.float32), -5.0, 5.0)
    growth = image_growth(TOKENS, SEQ, 3.0)
    return noise * growth[:, None]


def draw_conditioning(key, part):
    key = jax.random.fold_in(key, 17)
    noise = 0.8 * jnp.clip(jax.random.normal(key, (IMAGES, D), jnp.float32), -4.0, 4.0)
    growth = image_growth(IMAGES, 1, 3.0)
    return noise * growth[:, None]


def draw_lengths(key, part):
    key = jax.random.fold_in(key, 23)
    key_len, key_pick = jax.random.split(key)
    group_size = IMG_DEV * N_TENSOR
    drawn = jax.random.randint(key_len, (IMAGES,), SEQ // 8, SEQ + 1)
    chosen = jax.random.randint(key_pick, (IMAGES // group_size,), 0, group_size)
    full_image = jnp.arange(IMAGES, dtype=jnp.int32) % group_size == jnp.repeat(chosen, group_size)
    return jnp.where(full_image, SEQ, drawn).astype(jnp.int32)


def draw_positions(key, part):
    key = jax.random.fold_in(key, 37)
    grid_widths = jax.random.randint(key, (IMAGES,), 2, max(3, SEQ // 4) + 1)
    grid_widths = grid_widths.at[0].set(2)
    token_index = jnp.arange(SEQ, dtype=jnp.int32)
    row_index = token_index[None, :] // grid_widths[:, None]
    col_index = token_index[None, :] % grid_widths[:, None]
    return jnp.stack([row_index.reshape(-1), col_index.reshape(-1)]).astype(jnp.int32)


def set_ends(array, own_key, low, largest):
    shape = array.shape
    place = [jax.random.randint(jax.random.fold_in(own_key, axis), (), 0, shape[axis]) for axis in range(len(shape))]
    array = array.at[tuple(place)].set(low)
    longest = shape.index(max(shape))
    place[longest] = (place[longest] + 1) % shape[longest]
    return array.at[tuple(place)].set(largest)


def levels(rng, extent, cuts, least, high):
    factor_of = 1.0
    for position, blocks in cuts:
        draws = jax.random.uniform(jax.random.fold_in(jax.random.fold_in(rng, 6), position), (blocks,), jnp.float32, least / len(cuts), high / len(cuts))
        factor_of = factor_of * jnp.repeat(jnp.exp(draws), extent[position] // blocks).reshape((-1,) + (1,) * (len(extent) - 1 - position))
    return factor_of


def scatter_about(stream_key, dims, scale, limit, cuts=(), kind=jnp.bfloat16):
    array = scale * jax.random.normal(stream_key, dims, jnp.float32)
    if cuts:
        array = array * levels(stream_key, dims, cuts, -0.22, 0.18)
    return jnp.clip(array, -limit, limit).astype(kind)


def setup_inputs(seed: int = 0) -> dict:
    key_of = jax.random.split(jax.random.key(seed), 15)
    return {
        "patches": draw_patches(jax.random.fold_in(key_of[14], 71), 0),
        "conditioning": draw_conditioning(jax.random.fold_in(key_of[14], 71), 0),
        "time_bins": set_ends(jax.random.randint(key_of[2], (IMAGES,), 0, BINS), jax.random.fold_in(key_of[2], 1), 0, BINS - 1).astype(jnp.int32),
        "lengths": draw_lengths(jax.random.fold_in(key_of[14], 71), 0),
        "positions": draw_positions(jax.random.fold_in(key_of[14], 71), 0),
        "time_table": scatter_about(key_of[5], (BINS, D), 0.5, 3.0, (), jnp.float32),
        "w_ada": scatter_about(key_of[6], (D, 6 * D), D ** -0.5, 0.1875),
        "b_ada": scatter_about(key_of[7], (6 * D,), 0.5, 3.0, (), jnp.float32),
        "w_qkv": scatter_about(key_of[8], (D, 3, D), D ** -0.5, 0.1875, ((2, 4),)),
        "w_out": scatter_about(key_of[9], (D, D), (D // 16) ** -0.5, 0.75, ((0, 4),)),
        "branch_bias": scatter_about(key_of[10], (2 * D,), 0.3, 2.0, (), jnp.float32),
        "w_gu": scatter_about(key_of[11], (D, 2, FF), D ** -0.5, 0.1875, ((2, 4),)),
        "w_down": scatter_about(key_of[12], (FF, D), FF ** -0.5, 0.109375, ((0, 4),)),
        "d_out": scatter_about(key_of[13], (TOKENS, D), 1.0, 6.0, ((0, 32),), jnp.float32),
    }


EXACT = lax.Precision.HIGHEST
EPSILON = 1e-06

@jax.custom_vjp
def low(v):
    return lax.optimization_barrier(v.astype(jnp.bfloat16)).astype(jnp.float32)

@jax.custom_vjp
def low_back(v):
    return v

def low_keep(v):
    return (low(v), None)

def low_pass(kept, grad):
    return (grad,)

def back_keep(v):
    return (v, None)

def back_low(kept, grad):
    return (low(grad),)
low.defvjp(low_keep, low_pass)
low_back.defvjp(back_keep, back_low)

def layer_norm(values):
    centered = values - lax.optimization_barrier(jnp.mean(values, axis=-1, keepdims=True))
    return centered * lax.rsqrt(lax.optimization_barrier(jnp.mean(centered * centered, axis=-1, keepdims=True)) + EPSILON)

def rotate(vector, row_pos, col_pos):
    quarter = vector.shape[-1] // 4
    frequency = 10000.0 ** (-jnp.arange(quarter, dtype=jnp.float32) / quarter)
    angle_row = row_pos[:, None, None] * frequency
    angle_col = col_pos[:, None, None] * frequency
    cos_row, sin_row = (jnp.cos(angle_row), jnp.sin(angle_row))
    cos_col, sin_col = (jnp.cos(angle_col), jnp.sin(angle_col))
    part_one = vector[..., :quarter]
    part_two = vector[..., quarter:2 * quarter]
    part_three = vector[..., 2 * quarter:3 * quarter]
    part_four = vector[..., 3 * quarter:]
    return jnp.concatenate([part_one * cos_row - part_two * sin_row, part_two * cos_row + part_one * sin_row, part_three * cos_col - part_four * sin_col, part_four * cos_col + part_three * sin_col], axis=-1)

def block_forward(x_block, cond_block, time_table, w_ada, b_ada, w_qkv, w_out, branch_bias, w_gu, w_down, onehot, valid_mask, row_pos, col_pos):
    block_images = cond_block.shape[0]
    token_rows = block_images * SEQ
    cond_vec = cond_block + jnp.dot(onehot, time_table, precision=EXACT)
    silu_low = low(jax.nn.silu(cond_vec))
    modulation = (low_back(jnp.dot(silu_low, w_ada, precision=EXACT)) + b_ada).reshape(block_images, 6, 1, D)
    shift_one = modulation[:, 0]
    scale_one = modulation[:, 1]
    gate_one = modulation[:, 2]
    shift_two = modulation[:, 3]
    scale_two = modulation[:, 4]
    gate_two = modulation[:, 5]
    row_mask = valid_mask[:, :, None]
    inputs = x_block.reshape(block_images, SEQ, D)
    attn_in = low(layer_norm(inputs) * (1.0 + scale_one) + shift_one).reshape(token_rows, D)
    projected = low_back(jnp.dot(attn_in, w_qkv.reshape(D, 3 * D), precision=EXACT)).reshape(token_rows, 3, H, HD)
    head_shape = (block_images, SEQ, H, HD)
    queries = low(rotate(projected[:, 0], row_pos, col_pos)).reshape(head_shape)
    keys_low = low(rotate(projected[:, 1], row_pos, col_pos)).reshape(head_shape)
    values_low = low(projected[:, 2]).reshape(head_shape)
    scores = low_back(jnp.einsum('bqhd,bkhd->bhqk', queries, keys_low, precision=EXACT) * HD ** (-0.5))
    scores = jnp.where(valid_mask[:, None, None, :] > 0.5, scores, -1e+30)
    attn_probs = low(jax.nn.softmax(scores, axis=-1))
    attended = low(low_back(jnp.einsum('bhqk,bkhd->bqhd', attn_probs, values_low, precision=EXACT)))
    attended = attended.reshape(token_rows, D)
    attn_branch = (low_back(jnp.dot(attended, w_out, precision=EXACT)) + branch_bias[:D]).reshape(block_images, SEQ, D)
    attn_gated = row_mask * gate_one * attn_branch
    residual = inputs + attn_gated
    mlp_in = low(layer_norm(residual) * (1.0 + scale_two) + shift_two).reshape(token_rows, D)
    gate_up = low_back(jnp.dot(mlp_in, w_gu.reshape(D, 2 * FF), precision=EXACT)).reshape(token_rows, 2, FF)
    hidden = low(jax.nn.silu(gate_up[:, 0]) * gate_up[:, 1])
    mlp_branch = (low_back(jnp.dot(hidden, w_down, precision=EXACT)) + branch_bias[D:]).reshape(block_images, SEQ, D)
    mlp_gated = row_mask * gate_two * mlp_branch
    output = residual + mlp_gated
    square_sums = (jnp.sum(row_mask * inputs * inputs), jnp.sum(attn_gated * attn_gated), jnp.sum(mlp_gated * mlp_gated))
    return (output.reshape(token_rows, D), square_sums)

def reference(patches, conditioning, time_bins, lengths, positions, time_table, w_ada, b_ada, w_qkv, w_out, branch_bias, w_gu, w_down, d_out):
    block_images = math.gcd(IMAGES, max(1, 4096 // SEQ))
    block_count = IMAGES // block_images
    block_rows = block_images * SEQ
    params = (time_table, w_ada.astype(jnp.float32), b_ada, w_qkv.astype(jnp.float32), w_out.astype(jnp.float32), branch_bias, w_gu.astype(jnp.float32), w_down.astype(jnp.float32))
    blocks = (patches.reshape(block_count, block_rows, D), conditioning.reshape(block_count, block_images, D), time_bins.reshape(block_count, block_images), lengths.reshape(block_count, block_images), positions.reshape(2, block_count, block_rows).transpose(1, 0, 2), d_out.reshape(block_count, block_rows, D))

    def scan_step(totals, block_data):
        x_block, cond_block, bin_block, length_block, pos_block, grad_block = block_data
        onehot = (bin_block[:, None] == jnp.arange(BINS, dtype=jnp.int32)[None, :]).astype(jnp.float32)
        valid_mask = (jnp.arange(SEQ, dtype=jnp.int32)[None, :] < length_block[:, None]).astype(jnp.float32)
        row_pos = pos_block[0].astype(jnp.float32)
        col_pos = pos_block[1].astype(jnp.float32)

        def forward(x_in, c_in, *weights):
            return block_forward(x_in, c_in, *weights, onehot, valid_mask, row_pos, col_pos)
        outputs, pull_back, square_sums = jax.vjp(forward, x_block, cond_block, *params, has_aux=True)
        gradients = pull_back(grad_block)
        totals = tuple((total + grad for total, grad in zip(totals, gradients[2:])))
        return (totals, (outputs, gradients[0], gradients[1], jnp.stack(square_sums)))
    zero_grads = tuple((jnp.zeros(param.shape, jnp.float32) for param in params))
    totals, (outputs, d_inputs, d_conds, square_sums) = lax.scan(scan_step, zero_grads, blocks)
    token_total = jnp.sum(lengths).astype(jnp.float32) * D
    rms = jnp.sqrt(lax.optimization_barrier(jnp.sum(square_sums, axis=0)) / token_total)
    return (outputs.reshape(TOKENS, D), d_inputs.reshape(TOKENS, D), d_conds.reshape(IMAGES, D), totals[3], totals[4], totals[6], totals[7], totals[1], totals[2], totals[5], totals[0], rms)
```

```python
import functools

import jax
import jax.numpy as jnp
import numpy as np
from jax import lax
from jax.experimental import pallas as pl
from jax.experimental.pallas import tpu as pltpu
from jax.sharding import Mesh
from jax.sharding import PartitionSpec as P

HD = 72
EXACT = lax.Precision.HIGHEST
EPSILON = 1e-06
NEG = -1e30
VMEM_LIMIT = 58 * 1024 * 1024
UNROLL = 4
BF = jnp.bfloat16
F32 = jnp.float32
NT = (((1,), (1,)), ((), ()))
TN = (((0,), (0,)), ((), ()))


def dot(a, b):
    return jnp.dot(a, b, preferred_element_type=F32)


def dot_nt(a, b):
    return lax.dot_general(a, b, NT, preferred_element_type=F32)


def dot_tn(a, b):
    return lax.dot_general(a, b, TN, preferred_element_type=F32)


def call(kernel, name, grid, ins, outs, scratch=(), scalars=(), flops=0, moved=0, exps=0, deps=()):
    def spec(shape, block, index):
        if block is None:
            return pl.BlockSpec(shape, lambda *_: (0,) * len(shape))
        return pl.BlockSpec(block, lambda *at: index(*at[: len(grid)]))

    arrays = [item[0] for item in ins]
    in_specs = [spec(item[0].shape, item[1], item[2]) for item in ins]
    out_specs = [spec(item[0].shape, item[1], item[2]) for item in outs]
    count_s, count_i, count_d = len(scalars), len(ins), len(deps)

    def body(*refs):
        kept = refs[: count_s + count_i] + refs[count_s + count_i + count_d :]
        kernel(*kept)

    return pl.pallas_call(
        body,
        grid_spec=pltpu.PrefetchScalarGridSpec(
            num_scalar_prefetch=count_s,
            grid=grid,
            in_specs=in_specs + [pl.BlockSpec(memory_space=pl.ANY)] * count_d,
            out_specs=out_specs,
            scratch_shapes=list(scratch),
        ),
        out_shape=[item[0] for item in outs],
        compiler_params=pltpu.CompilerParams(
            dimension_semantics=("arbitrary",) * len(grid), vmem_limit_bytes=VMEM_LIMIT
        ),
        cost_estimate=pl.CostEstimate(flops=flops, bytes_accessed=moved, transcendentals=exps),
        name=name,
    )(*scalars, *arrays, *deps)


def shape(dims, dtype):
    return jax.ShapeDtypeStruct(tuple(dims), dtype)


def swap_matrix(width):
    quarter = HD // 4
    out = np.zeros((width, width), np.float32)
    for lane in range(width):
        if (lane % HD) % (2 * quarter) < quarter:
            out[lane + quarter, lane] = -1.0
        else:
            out[lane - quarter, lane] = 1.0
    return out


def head_mask(heads, which, dtype):
    lane = lax.broadcasted_iota(jnp.int32, (1, heads * HD), 1)
    inside = (lane >= which * HD) & (lane < (which + 1) * HD)
    return jnp.where(inside, 1.0, 0.0).astype(F32).astype(dtype)


def pick_weight(step, refs, scratch, last=None):
    for r, ref in enumerate(refs):

        @pl.when(step == r)
        def _(ref=ref):
            blocks, part = ref.shape[:2]
            for b in range(blocks):
                if last is not None and b == blocks - 1:
                    last[...] = ref[b]
                else:
                    scratch[b * part : (b + 1) * part, :] = ref[b]


def add_into(step, acc, rows, part):
    @pl.when(step == 0)
    def _():
        acc[rows, :] = part

    @pl.when(step > 0)
    def _():
        acc[rows, :] = acc[rows, :] + part


def hand_out(acc, own_ref, peer_ref):
    @pl.when(pl.program_id(0) == pl.num_programs(0) - 1)
    def _():
        half = own_ref.shape[0]
        own_ref[...] = acc[:half, :]
        peer_ref[...] = acc[half:, :].astype(BF)


def rows_of(step, count, body):
    for r in range(count):

        @pl.when(step == r)
        def _(r=r):
            body(r)


def copy_blocks(ref, blocks, scratch, first):
    part = ref.shape[1]
    for j, b in enumerate(blocks):
        scratch[first + j * part : first + (j + 1) * part, :] = ref[b]


def finish(left, right, own_ref, peer_ref, tile):
    half = own_ref.shape[0]
    for t in range(half // tile):
        at = slice(t * tile, (t + 1) * tile)
        own_ref[at, :] = dot_tn(left[:, at], right[...])
    for t in range(half // tile):
        there = slice(half + t * tile, half + (t + 1) * tile)
        peer_ref[t * tile : (t + 1) * tile, :] = dot_tn(left[:, there], right[...]).astype(BF)


def attn_fwd(lens, a_all, weights, cos, sin, heads, seq, deps=()):
    count, (rows, width), hw = len(weights), a_all.shape, heads * HD
    images = rows // seq
    scale = HD ** (-0.5)

    def kernel(lens, a_ref, cos_ref, sin_ref, swap_ref, *refs):
        w_refs, refs = refs[:count], refs[count:]
        q_ref, k_ref, v_ref, o_ref, own_ref, peer_ref, wcat, wout, full, o_all = refs
        step = pl.program_id(0)

        def pick(r):
            copy_blocks(w_refs[r], (0, 1, 2), wcat, 0)
            copy_blocks(w_refs[r], (3,), wout, r * hw)

        rows_of(step, count, pick)
        wcat[3 * hw :, :] = dot(swap_ref[...], wcat[: 2 * hw, :]).astype(BF)
        full[...] = dot_nt(wcat[...], a_ref[...])

        def image(i, carry):
            at = pl.ds(pl.multiple_of(i * seq, seq), seq)
            cos, sin = cos_ref[:, at], sin_ref[:, at]
            ok = lax.broadcasted_iota(jnp.int32, (seq, 1), 0) < lens[i]
            outs = []
            for h in range(heads):
                part = lambda j: full[j * hw + h * HD : j * hw + (h + 1) * HD, at]
                q = (part(0) * cos + part(3) * sin).astype(BF)
                k = (part(1) * cos + part(4) * sin).astype(BF)
                v = part(2).astype(BF)
                q_ref[0, h, :, at] = q
                k_ref[0, h, :, at] = k
                v_ref[0, h, :, at] = v
                st = jnp.where(ok, dot_tn(k, q) * scale, NEG)
                ex = jnp.exp(st - jnp.max(st, axis=0, keepdims=True))
                probs = (ex * (1.0 / jnp.sum(ex, axis=0, keepdims=True))).astype(BF)
                outs.append(dot(v, probs))
            o_ref[0, :, at] = jnp.concatenate(outs, axis=0).astype(BF)
            return carry

        lax.fori_loop(0, images, image, 0, unroll=UNROLL)

        def keep(r):
            o_all[r * hw : (r + 1) * hw, :] = o_ref[0]

        rows_of(step, count, keep)

        @pl.when(step == count - 1)
        def _():
            finish(o_all, wout, own_ref, peer_ref, seq)

    head = (shape((count, heads, HD, rows), BF), (1, heads, HD, rows), lambda z: (z, 0, 0, 0))
    return call(
        kernel,
        "attn_fwd",
        (count,),
        [(x, None, None) for x in (a_all, cos, sin, jnp.asarray(swap_matrix(2 * hw).T, BF))]
        + [(w, None, None) for w in weights],
        [
            head,
            head,
            head,
            (shape((count, hw, rows), BF), (1, hw, rows), lambda z: (z, 0, 0)),
            (shape((rows // 2, width), F32), None, None),
            (shape((rows // 2, width), BF), None, None),
        ],
        scratch=[
            pltpu.VMEM((5 * hw, width), BF),
            pltpu.VMEM((count * hw, width), BF),
            pltpu.VMEM((5 * hw, rows), F32),
            pltpu.VMEM((count * hw, rows), BF),
        ],
        scalars=(lens,),
        flops=2 * count * rows * width * 6 * hw + 8 * count * rows * heads * seq * 256,
        moved=20_000_000,
        exps=count * rows * heads * seq,
        deps=deps,
    )


def attn_bwd(lens, da_all, weights, cos, sin, q, k, v, heads, seq, deps=()):
    count, (rows, width), hw = len(weights), da_all.shape, heads * HD
    images = rows // seq
    scale = HD ** (-0.5)

    def kernel(lens, da_ref, cos_ref, sin_ref, swap_ref, q_ref, k_ref, v_ref, *refs):
        w_refs, refs = refs[:count], refs[count:]
        dqkv_ref, own_ref, peer_ref, w_all, wout, do_all, d_all = refs
        step = pl.program_id(0)

        def pick(r):
            copy_blocks(w_refs[r], (0, 1, 2), w_all, r * 3 * hw)
            copy_blocks(w_refs[r], (3,), wout, 0)

        rows_of(step, count, pick)
        do_all[...] = dot_nt(wout[...], da_ref[...])

        def image(i, carry):
            at = pl.ds(pl.multiple_of(i * seq, seq), seq)
            cos, sin = cos_ref[:, at], sin_ref[:, at]
            ok = lax.broadcasted_iota(jnp.int32, (seq, 1), 0) < lens[i]
            dqs, dks, dvs = [], [], []
            for h in range(heads):
                do = do_all[h * HD : (h + 1) * HD, at].astype(BF)
                q, k, v = q_ref[0, h, :, at], k_ref[0, h, :, at], v_ref[0, h, :, at]
                st = jnp.where(ok, dot_tn(k, q) * scale, NEG)
                dp = dot_tn(v, do)
                ex = jnp.exp(st - jnp.max(st, axis=0, keepdims=True))
                probs = ex * (1.0 / jnp.sum(ex, axis=0, keepdims=True))
                inner = jnp.sum(dp * probs, axis=0, keepdims=True)
                ds = (probs * (dp - inner)).astype(BF)
                dvs.append(dot_nt(do, probs.astype(BF)))
                dk = dot_nt(q, ds), dot_nt(dot(swap_ref[...], q).astype(BF), ds)
                dq = dot(k, ds), dot(dot(swap_ref[...], k).astype(BF), ds)
                dqs.append((dq[0] * cos - dq[1] * sin) * scale)
                dks.append((dk[0] * cos - dk[1] * sin) * scale)
            dqkv_ref[0, :, at] = jnp.concatenate(dqs + dks + dvs, axis=0).astype(BF)
            return carry

        lax.fori_loop(0, images, image, 0, unroll=UNROLL)

        def keep(r):
            d_all[r * 3 * hw : (r + 1) * 3 * hw, :] = dqkv_ref[0]

        rows_of(step, count, keep)

        @pl.when(step == count - 1)
        def _():
            finish(d_all, w_all, own_ref, peer_ref, seq)

    head = lambda x: (x, (1, heads, HD, rows), lambda z: (z, 0, 0, 0))
    return call(
        kernel,
        "attn_bwd",
        (count,),
        [(x, None, None) for x in (da_all, cos, sin, jnp.asarray(swap_matrix(HD).T, BF))]
        + [head(q), head(k), head(v)]
        + [(w, None, None) for w in weights],
        [
            (shape((count, 3 * hw, rows), BF), (1, 3 * hw, rows), lambda z: (z, 0, 0)),
            (shape((rows // 2, width), F32), None, None),
            (shape((rows // 2, width), BF), None, None),
        ],
        scratch=[
            pltpu.VMEM((count * 3 * hw, width), BF),
            pltpu.VMEM((hw, width), BF),
            pltpu.VMEM((hw, rows), F32),
            pltpu.VMEM((count * 3 * hw, rows), BF),
        ],
        scalars=(lens,),
        flops=2 * count * rows * width * 4 * hw + 20 * count * rows * heads * seq * 256,
        moved=20_000_000,
        exps=count * rows * heads * seq,
        deps=deps,
    )


def tiles(total, tile, body):
    def step(i, carry):
        body(pl.ds(pl.multiple_of(i * tile, tile), tile))
        return carry

    lax.fori_loop(0, total // tile, step, 0)


def mlp_fwd(a_all, weights, deps=()):
    count, (rows, width) = len(weights), a_all.shape
    cols = weights[0].shape[0] * weights[0].shape[1]
    units = cols // 2

    def kernel(a_ref, *refs):
        w_refs, (gu_ref, hid_ref, wcat) = refs[:count], refs[count:]
        pick_weight(pl.program_id(0), w_refs, wcat)

        def block(at):
            gu = dot_nt(a_ref[at, :], wcat[...])
            gu_ref[0, at, :] = gu
            g, u = gu[:, :units], gu[:, units:]
            hid_ref[0, at, :] = (g * jax.nn.sigmoid(g) * u).astype(BF)

        tiles(rows, 256, block)

    each = lambda z: (z, 0, 0)
    return call(
        kernel,
        "mlp_fwd",
        (count,),
        [(a_all, None, None)] + [(w, None, None) for w in weights],
        [
            (shape((count, rows, cols), F32), (1, rows, cols), each),
            (shape((count, rows, units), BF), (1, rows, units), each),
        ],
        scratch=[pltpu.VMEM((cols, width), BF)],
        flops=2 * count * rows * width * cols,
        moved=26_000_000,
        exps=count * rows * units,
        deps=deps,
    )


def mlp_bwd(dm_all, downs, gus, gate_up, deps=()):
    count, (rows, width) = len(gus), dm_all.shape
    cols = gus[0].shape[0] * gus[0].shape[1]
    units = cols // 2

    def kernel(dm_ref, gu_ref, *refs):
        d_refs, g_refs, refs = refs[:count], refs[count : 2 * count], refs[2 * count :]
        dgu_ref, own_ref, peer_ref, wd, wgu, acc = refs
        step = pl.program_id(0)
        pick_weight(step, d_refs, wd)
        pick_weight(step, g_refs, wgu)

        def block(at):
            dhid = dot_nt(dm_ref[at, :], wd[...])
            g, u = gu_ref[0, at, :units], gu_ref[0, at, units:]
            sig = jax.nn.sigmoid(g)
            dg = dhid * u * sig * (1.0 + g * (1.0 - sig))
            du = dhid * g * sig
            low = jnp.concatenate([dg, du], axis=1).astype(BF)
            dgu_ref[0, at, :] = low
            add_into(step, acc, at, dot(low, wgu[...]))

        tiles(rows, 256, block)
        hand_out(acc, own_ref, peer_ref)

    each = lambda z: (z, 0, 0)
    return call(
        kernel,
        "mlp_bwd",
        (count,),
        [(dm_all, None, None), (gate_up, (1, rows, cols), each)]
        + [(w, None, None) for w in downs + gus],
        [
            (shape((count, rows, cols), BF), (1, rows, cols), each),
            (shape((rows // 2, width), F32), None, None),
            (shape((rows // 2, width), BF), None, None),
        ],
        scratch=[
            pltpu.VMEM((units, width), BF),
            pltpu.VMEM((cols, width), BF),
            pltpu.VMEM((rows, width), F32),
        ],
        flops=3 * count * rows * width * cols,
        moved=30_000_000,
        exps=count * rows * units,
        deps=deps,
    )


def mlp_out(hidden, downs, deps=()):
    count, rows, units = hidden.shape
    width = downs[0].shape[2]

    def kernel(hid_ref, *refs):
        d_refs, (own_ref, peer_ref, wd, acc) = refs[:count], refs[count:]
        step = pl.program_id(0)
        pick_weight(step, d_refs, wd)
        tiles(rows, 256, lambda at: add_into(step, acc, at, dot(hid_ref[0, at, :], wd[...])))
        hand_out(acc, own_ref, peer_ref)

    return call(
        kernel,
        "mlp_out",
        (count,),
        [(hidden, (1, rows, units), lambda z: (z, 0, 0))] + [(w, None, None) for w in downs],
        [
            (shape((rows // 2, width), F32), None, None),
            (shape((rows // 2, width), BF), None, None),
        ],
        scratch=[pltpu.VMEM((units, width), BF), pltpu.VMEM((rows, width), F32)],
        flops=2 * count * rows * width * units,
        moved=12_000_000,
        deps=deps,
    )


ROLES = ((1, 3), (0, 2), (2, 3), (0, 1))


def grad_split(place, pairs, deps=()):
    rows, width = pairs[0][0].shape
    count = pairs[0][1].shape[0]
    last = [right.shape[2] == rows for _, right in pairs]
    widths = [right.shape[1 if flip else 2] for (_, right), flip in zip(pairs, last)]
    cols, strip = sum(widths), width // 8

    def kernel(place, *refs):
        n = len(pairs)
        lefts, rights, outs, refs = refs[:n], refs[n : 2 * n], refs[2 * n : 2 * n + 4], refs[2 * n + 4 :]
        turned, res = refs[:n], refs[n]

        @pl.when(pl.program_id(0) == 0)
        def _():
            for left, lt in zip(lefts, turned):
                lt[...] = left[...].T

        begin = 0
        for lt, right, size, flip in zip(turned, rights, widths, last):
            part = dot_nt(lt[...], right[0]) if flip else dot(lt[...], right[0])
            res[:, begin : begin + size] = part
            begin += size
        for core, ref, blocks in zip((0, 0, 1, 1), outs, ROLES):
            for j, rel in enumerate(blocks):
                first = ((place[0] ^ rel) * 2 + (place[1] ^ core)) * strip
                ref[0, j] = res[pl.ds(pl.multiple_of(first, 16), strip), :].astype(BF)

    return call(
        kernel,
        "grad_split",
        (count,),
        [(left, None, None) for left, _ in pairs]
        + [(right, (1,) + right.shape[1:], lambda z: (z, 0, 0)) for _, right in pairs],
        [(shape((count, 2, strip, cols), BF), (1, 2, strip, cols), lambda z: (z, 0, 0, 0))] * 4,
        scratch=[pltpu.VMEM((width, rows), BF)] * len(pairs) + [pltpu.VMEM((width, cols), F32)],
        scalars=(place,),
        flops=2 * count * rows * width * cols,
        moved=2 * rows * width + 2 * count * rows * cols + 2 * count * width * cols,
        deps=deps,
    )


def assemble(place, near, first_x, second_y, first_y, second_x, deps=()):
    part, width = near.shape
    half = first_x.shape[0]

    def kernel(place, near, fx, sy, fy, sx, out):
        q = place[0]
        out[q] = near[...]
        out[q ^ 1, :half] = fx[...]
        out[q ^ 1, half:] = sx[0]
        out[q ^ 2, :half] = fy[0]
        out[q ^ 2, half:] = sy[...]
        out[q ^ 3, :half] = fy[1]
        out[q ^ 3, half:] = sx[1]

    return call(
        kernel,
        "assemble",
        (1,),
        [(x, None, None) for x in (near, first_x, second_y, first_y, second_x)],
        [(shape((4, part, width), BF), None, None)],
        scalars=(place,),
        moved=16 * part * width,
        deps=deps,
    )[0]


def norm(x):
    centered = x - jnp.mean(x, axis=-1, keepdims=True)
    inverse = lax.rsqrt(jnp.mean(centered * centered, axis=-1, keepdims=True) + EPSILON)
    return centered * inverse, inverse


def norm_back(d_normed, normed, inverse, scale):
    d_hat = d_normed * (1.0 + scale)
    return inverse * (
        d_hat
        - jnp.mean(d_hat, axis=-1, keepdims=True)
        - normed * jnp.mean(d_hat * normed, axis=-1, keepdims=True)
    )


def total(x):
    return jnp.sum(x, axis=0, keepdims=True)


SHIFT_ONE, SCALE_ONE, GATE_ONE, SHIFT_TWO, SCALE_TWO, GATE_TWO = range(6)


def by_image(body, name, lengths, mod, rows_in, bias, outs, sums, deps=()):
    images, _, width = mod.shape
    seq = rows_in[0].shape[0] // images
    count = len(rows_in)

    def kernel(lens, mod_ref, bias_ref, *refs):
        row_id = lax.broadcasted_iota(jnp.int32, (seq, 1), 0)
        mask = jnp.where(row_id < lens[pl.program_id(0)], 1.0, 0.0).astype(F32)
        values = [ref[...].astype(F32) for ref in refs[:count]]
        got = body(mask, [mod_ref[0, j : j + 1, :] for j in range(6)], bias_ref[...], *values)
        for ref, value in zip(refs[count:-1], got):
            ref[...] = value.astype(ref.dtype)
        for j, value in enumerate(got[len(outs) :]):
            refs[-1][0, j : j + 1, :] = value

    block = ((seq, width), lambda i: (i, 0))
    return call(
        kernel,
        name,
        (images,),
        [(mod, (1, 6, width), lambda i: (i, 0, 0)), (bias, None, None)]
        + [(x,) + block for x in rows_in],
        [(shape(rows_in[0].shape, dtype),) + block for dtype in outs]
        + [(shape((images, sums, width), F32), (1, sums, width), lambda i: (i, 0, 0))],
        scalars=(lengths,),
        flops=30 * seq * width * images,
        moved=sum(x.size * x.dtype.itemsize for x in rows_in) + 4 * seq * width * images,
        deps=deps,
    )


def pre_attention(mask, mod, bias, x, upstream):
    normed, _ = norm(x)
    dm = mask * mod[GATE_TWO] * upstream
    return normed * (1.0 + mod[SCALE_ONE]) + mod[SHIFT_ONE], dm, total(dm), total(mask * x * x)


def pre_mlp(mask, mod, bias, x, att_own, att_peer):
    gated = mask * mod[GATE_ONE] * (att_own + att_peer + bias)
    residual = x + gated
    normed, _ = norm(residual)
    return residual, normed * (1.0 + mod[SCALE_TWO]) + mod[SHIFT_TWO], total(gated * gated)


def post_mlp(mask, mod, bias, residual, upstream, mlp_own, mlp_peer):
    branch = mlp_own + mlp_peer + bias
    gated = mask * mod[GATE_TWO] * branch
    return residual + gated, total(mask * branch * upstream), total(gated * gated)


def back_mlp(mask, mod, bias, residual, upstream, att_own, att_peer, da_own, da_peer):
    normed, inverse = norm(residual)
    da = da_own + da_peer
    dh = upstream + norm_back(da, normed, inverse, mod[SCALE_TWO])
    d_att = mask * mod[GATE_ONE] * dh
    branch = att_own + att_peer + bias
    return dh, d_att, total(mask * branch * dh), total(da), total(da * normed), total(d_att)


def back_attention(mask, mod, bias, x, dh, da_own, da_peer):
    normed, inverse = norm(x)
    da = da_own + da_peer
    return dh + norm_back(da, normed, inverse, mod[SCALE_ONE]), total(da), total(da * normed)


def ring(count, shift):
    return [(i, (i + shift) % count) for i in range(count)]


def take(array, index, axis):
    return lax.dynamic_index_in_dim(array, index, axis, keepdims=False)


def local(
    sizes,
    patches,
    conditioning,
    time_bins,
    lengths,
    positions,
    time_table,
    w_ada,
    b_ada,
    w_qkv,
    w_out,
    branch_bias,
    w_gu,
    w_down,
    d_out,
):
    axes = tuple(sizes)
    ny, nx, nc, tn = sizes.values()
    square = nx == 2 and ny == 2
    at_y, at_x, at_c, at_z = (lax.axis_index(name) for name in axes)
    at_q = at_y * nx + at_x
    devices = ny * nx * nc * tn
    image_count, width = conditioning.shape
    rows = patches.shape[0]
    seq = rows // image_count
    heads = w_qkv.shape[2] // HD // nc
    hw = heads * HD
    units = w_gu.shape[2] // nc
    strip = width // (ny * nx * nc)
    place = jnp.stack([at_q, at_c]).astype(jnp.int32)
    swap = ring(2, 1)

    def peer(value):
        return lax.ppermute(value, "c", ring(nc, 1))

    def core_share(weight, axis):
        size = weight.shape[axis] // nc
        return lax.dynamic_slice_in_dim(weight, at_c * size, size, axis)

    def after(value, *others):
        return lax.optimization_barrier((value, others))[0] if others else value

    flow = {"z": [], "plane": []}

    def weight_gather(base, batches):
        if not square:
            flat = base.reshape(ny * nx, -1, width)
            piece = take(flat, at_q, 0)
            got = [lax.ppermute(piece, "z", ring(tn, r)) for r in range(1, tn)]
            whole = lax.all_gather(jnp.stack(got), ("y", "x"), axis=1)
            return [base] + [whole[r].reshape(base.shape) for r in range(tn - 1)]
        part = base.shape[1]
        half = part // 32 * 16
        piece = after(take(base, at_q, 0), *flow["z"])
        near = [lax.ppermute(piece, "z", ring(tn, r)) for r in range(1, tn)]
        flow["z"] = near
        out = [base]
        for batch in batches:
            mine = [near[r - 1] for r in batch]
            mine = after(mine, *flow["plane"])
            first = jnp.stack([x[:half] for x in mine])
            second = jnp.stack([x[half:] for x in mine])
            first_x = lax.ppermute(first, "x", swap)
            second_y = lax.ppermute(second, "y", swap)
            first_y = lax.ppermute(jnp.stack([first, first_x], axis=1), "y", swap)
            second_x = lax.ppermute(jnp.stack([second, second_y], axis=1), "x", swap)
            flow["plane"] = [first_y, second_x]
            for j in range(len(batch)):
                out.append(
                    assemble(place, mine[j], first_x[j], second_y[j], first_y[j], second_x[j])
                )
        return out

    heads_own = jnp.concatenate(
        [core_share(w_qkv.transpose(1, 2, 0), 1), core_share(w_out, 0)[None]], axis=0
    )
    heads_all = weight_gather(heads_own, ((1,), (2, 3)))
    gu_own = core_share(w_gu.transpose(1, 2, 0), 1).reshape(4, units // 2, width)
    gu_all = weight_gather(gu_own, ((1, 2, 3),))
    down_all = weight_gather(core_share(w_down, 0).reshape(4, units // 4, width), ((1, 2, 3),))

    def grad_reduce(pairs, deps=()):
        if square:
            send_a, keep_a, send_b, keep_b = grad_split(place, pairs, deps)
            got_a = lax.ppermute(send_a, "x", swap)
            got_b = lax.ppermute(send_b, "y", swap)

            def part(keep, got, j):
                return keep[:, j].astype(F32) + got[:, j].astype(F32)

            got_a2 = lax.ppermute(part(keep_a, got_a, 1).astype(BF), "y", swap)
            got_b2 = lax.ppermute(part(keep_b, got_b, 1).astype(BF), "x", swap)
            mine = part(keep_a, got_a, 0) + got_a2.astype(F32)
            other = part(keep_b, got_b, 0) + got_b2.astype(F32)
        else:
            flip = lambda right: right.swapaxes(1, 2) if right.shape[2] == 2 * rows else right
            full = jnp.concatenate(
                [
                    jnp.einsum("rd,zrn->zdn", left, flip(right), preferred_element_type=F32)
                    for left, right in pairs
                ],
                axis=2,
            )
            full = full.astype(BF).reshape(tn, ny * nx, nc, strip, -1)
            summed = lax.psum_scatter(full, ("y", "x"), scatter_dimension=1, tiled=False)
            mine = take(summed, at_c, 1).astype(F32)
            other = take(summed, 1 - at_c, 1).astype(F32)
        blocks = jnp.stack([mine, other], axis=1)
        summed = blocks[0]
        for r in range(1, tn):
            sent = blocks[r].astype(BF)
            summed = summed + lax.ppermute(sent, "z", ring(tn, -r)).astype(F32)
        got = peer(summed[1].astype(BF)).astype(F32)
        own = summed[0]
        low, high = jnp.where(at_c == 0, own, got), jnp.where(at_c == 0, got, own)
        return low, high

    bins = jnp.arange(time_table.shape[0], dtype=jnp.int32)
    onehot = (time_bins[:, None] == bins[None, :]).astype(F32)
    cond_vec = conditioning + jnp.dot(onehot, time_table, precision=EXACT)
    cond_sig = jax.nn.sigmoid(cond_vec)
    silu_low = (cond_vec * cond_sig).astype(BF)
    mod = (dot(silu_low, w_ada) + b_ada).reshape(image_count, 6, width)
    bias_attn, bias_mlp = branch_bias[None, :width], branch_bias[None, width:]
    elementwise = functools.partial(by_image, lengths=lengths, mod=mod)
    a1_own, dm_own, sums_pre = elementwise(
        pre_attention, "pre_attention", rows_in=(patches, d_out), bias=bias_attn, outs=(BF, BF), sums=2
    )
    a1_all = jnp.concatenate([a1_own, peer(a1_own)], axis=0)
    dm_all = jnp.concatenate([dm_own, peer(dm_own)], axis=0)
    facts = jnp.concatenate([positions.reshape(-1), lengths])
    facts_peer = peer(facts)
    lens = jnp.concatenate([lengths, facts_peer[2 * rows :]])
    pos = jnp.concatenate([positions, facts_peer[: 2 * rows].reshape(2, rows)], axis=1).astype(F32)
    quarter = HD // 4
    frequency = 10000.0 ** (-jnp.arange(quarter, dtype=F32) / quarter)
    angle = pos[:, None, :] * frequency[None, :, None]
    cosine, sine = jnp.cos(angle), jnp.sin(angle)
    cos = jnp.concatenate([cosine[0], cosine[0], cosine[1], cosine[1]], axis=0)
    sin = jnp.concatenate([sine[0], sine[0], sine[1], sine[1]], axis=0)

    q, k, v, attended, att_own, att_peer = attn_fwd(
        lens, a1_all, heads_all, cos, sin, heads, seq
    )
    att = (att_own, peer(att_peer))
    residual, a2_own, sums_att = elementwise(
        pre_mlp, "pre_mlp", rows_in=(patches,) + att, bias=bias_attn, outs=(F32, BF), sums=1
    )
    a2_all = jnp.concatenate([a2_own, peer(a2_own)], axis=0)

    gate_up, hidden = mlp_fwd(a2_all, gu_all)
    down_low, down_high = grad_reduce([(dm_all, hidden)])
    d_gate_up, da2_own, da2_peer = mlp_bwd(dm_all, down_all, gu_all, gate_up)
    gu_low, gu_high = grad_reduce([(a2_all, d_gate_up)])
    dh, da_own, sums_back = elementwise(
        back_mlp,
        "back_mlp",
        rows_in=(residual, d_out) + att + (da2_own, peer(da2_peer)),
        bias=bias_attn,
        outs=(F32, BF),
        sums=4,
    )
    da_all = jnp.concatenate([da_own, peer(da_own)], axis=0)
    mlp_own, mlp_peer = mlp_out(hidden, down_all)
    output, sums_mlp = elementwise(
        post_mlp,
        "post_mlp",
        rows_in=(residual, d_out, mlp_own, peer(mlp_peer)),
        bias=bias_mlp,
        outs=(F32,),
        sums=2,
    )

    d_qkv, da1_own, da1_peer = attn_bwd(
        lens, da_all, heads_all, cos, sin, q, k, v, heads, seq
    )
    heads_low, heads_high = grad_reduce([(a1_all, d_qkv), (da_all, attended)])
    d_inputs, sums_one = elementwise(
        back_attention,
        "back_attention",
        rows_in=(patches, dh, da1_own, peer(da1_peer)),
        bias=bias_attn,
        outs=(F32,),
        sums=2,
    )

    d_mod = jnp.concatenate([sums_one, sums_back[:, :3], sums_mlp[:, :1]], axis=1)
    d_mod = d_mod.reshape(image_count, 6 * width)
    d_silu = dot_nt(d_mod.astype(BF), w_ada)
    d_cond = d_silu * cond_sig * (1.0 + cond_vec * (1.0 - cond_sig))
    d_bias = jnp.concatenate([jnp.sum(sums_back[:, 3], axis=0), jnp.sum(sums_pre[:, 0], axis=0)])
    sums = jnp.stack(
        [
            jnp.sum(sums_pre[:, 1]),
            jnp.sum(sums_att),
            jnp.sum(sums_mlp[:, 1]),
            jnp.sum(lengths).astype(F32),
        ]
    )
    ada_cols, bias_cols = 6 * width // devices, 2 * width // devices
    message = jnp.concatenate(
        [
            d_mod.reshape(image_count, devices, ada_cols).transpose(1, 0, 2).reshape(devices, -1),
            d_bias.reshape(devices, bias_cols),
            jnp.broadcast_to(sums[None], (devices, 4)),
        ],
        axis=1,
    )
    arrived = lax.all_to_all(message, axes, 0, 0, tiled=True)
    d_mod_all = arrived[:, : image_count * ada_cols].reshape(devices * image_count, ada_cols)
    rest = jnp.sum(arrived[:, image_count * ada_cols :], axis=0)
    grad_b_ada = jnp.sum(d_mod_all, axis=0)
    grad_bias = rest[:bias_cols]
    sums_all = rest[bias_cols:]
    rms_values = jnp.sqrt(sums_all[:3] / (sums_all[3] * width))
    facts = jnp.concatenate([d_cond, silu_low.astype(F32), time_bins[:, None].astype(F32)], axis=1)
    facts = jnp.broadcast_to(facts[None], (devices,) + facts.shape)
    facts_all = lax.all_to_all(facts, axes, 0, 0, tiled=True).reshape(devices * image_count, -1)
    d_cond_all, silu_all = facts_all[:, :width], facts_all[:, width : 2 * width].astype(BF)
    bins_all = facts_all[:, 2 * width].astype(jnp.int32)
    grad_ada = dot_tn(silu_all, d_mod_all.astype(BF))
    table_rows = time_table.shape[0] // devices
    flat = (at_q * nc + at_c) * tn + at_z
    own_bins = flat * table_rows + jnp.arange(table_rows, dtype=jnp.int32)
    picks = (own_bins[:, None] == bins_all[None, :]).astype(F32)
    grad_table = jnp.dot(picks, d_cond_all, precision=EXACT)

    def halves(low, high, parts):
        both = [value.reshape(strip, parts, -1) for value in (low, high)]
        return jnp.concatenate(both, axis=2)

    return (
        output,
        d_inputs,
        d_cond,
        halves(heads_low[:, : 3 * hw], heads_high[:, : 3 * hw], 3),
        halves(heads_low[:, 3 * hw :], heads_high[:, 3 * hw :], 1)[:, 0].T,
        halves(gu_low, gu_high, 2),
        halves(down_low, down_high, 1)[:, 0].T,
        grad_ada,
        grad_b_ada,
        grad_bias,
        grad_table,
        rms_values,
    )


def solution(mesh):
    groups, tn = mesh.shape["dp"], mesh.shape["tensor"]
    nc, nx = 2, 2
    sizes = {"y": groups // (nx * nc), "x": nx, "c": nc, "z": tn}
    fine = Mesh(mesh.devices.reshape(tuple(sizes.values())), tuple(sizes))
    dp = ("y", "x", "c")
    every = dp + ("z",)
    return jax.shard_map(
        functools.partial(local, sizes),
        mesh=fine,
        in_specs=(
            P(every, None),
            P(every, None),
            P(every),
            P(every),
            P(None, every),
            P(),
            P(),
            P(),
            P(None, None, "z"),
            P("z", None),
            P(),
            P(None, None, "z"),
            P("z", None),
            P(every, None),
        ),
        out_specs=(
            P(every, None),
            P(every, None),
            P(every, None),
            P(dp, None, "z"),
            P("z", dp),
            P(dp, None, "z"),
            P("z", dp),
            P(None, every),
            P(every),
            P(every),
            P(every, None),
            P(),
        ),
        check_vma=False,
    )
```

```python
import functools

import jax
import jax.numpy as jnp
import numpy as np
from jax import lax
from jax.experimental import pallas as pl
from jax.experimental.pallas import tpu as pltpu
from jax.sharding import Mesh
from jax.sharding import PartitionSpec as P

HD = 72
EXACT = lax.Precision.HIGHEST
EPSILON = 1e-06
NEG = -1e30
VMEM_LIMIT = 58 * 1024 * 1024
UNROLL = 4
MLP_TILE = 256
BF = jnp.bfloat16
F32 = jnp.float32
NT = (((1,), (1,)), ((), ()))
TN = (((0,), (0,)), ((), ()))


def dot(a, b):
    return jnp.dot(a, b, preferred_element_type=F32)


def dot_nt(a, b):
    return lax.dot_general(a, b, NT, preferred_element_type=F32)


def dot_tn(a, b):
    return lax.dot_general(a, b, TN, preferred_element_type=F32)


def call(kernel, name, grid, ins, outs, scratch=(), scalars=(), flops=0, moved=0, exps=0, deps=(), carry=(), dynamic=False):
    def spec(shape, block, index):
        if block is None:
            return pl.BlockSpec(shape, lambda *_: (0,) * len(shape))
        return pl.BlockSpec(block, index if dynamic else lambda *at: index(*at[: len(grid)]))

    arrays = [item[0] for item in ins]
    in_specs = [spec(item[0].shape, item[1], item[2]) for item in ins]
    out_specs = [spec(item[0].shape, item[1], item[2]) for item in outs]
    count_s, count_i, count_d = len(scalars), len(ins), len(deps) + len(carry)

    def body(*refs):
        kept = refs[: count_s + count_i] + refs[count_s + count_i + count_d :]
        kernel(*kept)

    return pl.pallas_call(
        body,
        grid_spec=pltpu.PrefetchScalarGridSpec(
            num_scalar_prefetch=count_s,
            grid=grid,
            in_specs=in_specs + [pl.BlockSpec(memory_space=pl.ANY)] * count_d,
            out_specs=out_specs,
            scratch_shapes=list(scratch),
        ),
        out_shape=[item[0] for item in outs],
        compiler_params=pltpu.CompilerParams(
            dimension_semantics=("arbitrary",) * len(grid), vmem_limit_bytes=VMEM_LIMIT
        ),
        cost_estimate=pl.CostEstimate(flops=flops, bytes_accessed=moved, transcendentals=exps),
        input_output_aliases={count_s + count_i + len(deps) + j: j for j in range(len(carry))},
        name=name,
    )(*scalars, *arrays, *deps, *carry)


def shape(dims, dtype):
    return jax.ShapeDtypeStruct(tuple(dims), dtype)


def swap_matrix(width):
    quarter = HD // 4
    out = np.zeros((width, width), np.float32)
    for lane in range(width):
        if (lane % HD) % (2 * quarter) < quarter:
            out[lane + quarter, lane] = -1.0
        else:
            out[lane - quarter, lane] = 1.0
    return out


def head_mask(heads, which, dtype):
    lane = lax.broadcasted_iota(jnp.int32, (1, heads * HD), 1)
    inside = (lane >= which * HD) & (lane < (which + 1) * HD)
    return jnp.where(inside, 1.0, 0.0).astype(F32).astype(dtype)


def finish(parts, outs, starts, tile):
    half = outs[0].shape[0]
    for j, ref in enumerate(outs):
        for t in range(half // tile):
            at = slice(t * tile, (t + 1) * tile)
            value = parts(slice(j * half + t * tile, j * half + (t + 1) * tile))
            if starts:
                value = value + starts[j][at, :]
            ref[at, :] = value.astype(ref.dtype)


def at_step(step, count, body):
    for r in range(count):

        @pl.when(step == r)
        def _(r=r):
            body(r)


def halves_out(rows, width, last):
    return [(shape((rows, width), F32), None, None), (shape((rows, width), BF if last else F32), None, None)]


def by_step(array, begin=0):
    return (array, (1,) + array.shape[1:], lambda z: (z + begin,) + (0,) * (array.ndim - 1))


def step_out(dims, dtype):
    return (shape(dims, dtype), (1,) + tuple(dims[1:]), lambda z: (z,) + (0,) * (len(dims) - 1))


def attn_fwd(lens, place, both, weights, count, total, carry, starts, cos, sin, heads, seq, deps=()):
    (half, width), hw = both[0].shape, heads * HD
    ahead = 1 if carry else 0
    last = bool(carry)
    rows = 2 * half
    images, given = rows // seq, len(starts)
    scale = HD ** (-0.5)

    def kernel(lens, place, own_in, peer_in, cos_ref, sin_ref, swap_ref, w_ref, *refs):
        starts, refs = refs[:given], refs[given:]
        q_ref, k_ref, v_ref, o_ref, own_ref, peer_ref, wcat, wout, full, o_all = refs
        step = pl.program_id(0)
        for j in range(3):
            wcat[j * hw : (j + 1) * hw, :] = w_ref[0, j]
        wcat[3 * hw :, :] = dot(swap_ref[...], wcat[: 2 * hw, :]).astype(BF)
        full[:, :half] = dot_nt(wcat[...], own_in[...])
        full[:, half:] = dot_nt(wcat[...], peer_in[...])

        def image(i, carry):
            at = pl.ds(pl.multiple_of(i * seq, seq), seq)
            cos, sin = cos_ref[:, at], sin_ref[:, at]
            ok = lax.broadcasted_iota(jnp.int32, (seq, 1), 0) < lens[i]
            outs = []
            for h in range(heads):
                part = lambda j: full[j * hw + h * HD : j * hw + (h + 1) * HD, at]
                q = (part(0) * cos + part(3) * sin).astype(BF)
                k = (part(1) * cos + part(4) * sin).astype(BF)
                v = part(2).astype(BF)
                q_ref[0, h, :, at] = q
                k_ref[0, h, :, at] = k
                v_ref[0, h, :, at] = v
                st = jnp.where(ok, dot_tn(k, q) * scale, NEG)
                ex = jnp.exp(st - jnp.max(st, axis=0, keepdims=True))
                probs = (ex * (1.0 / jnp.sum(ex, axis=0, keepdims=True))).astype(BF)
                outs.append(dot(v, probs))
            o_ref[0, :, at] = jnp.concatenate(outs, axis=0).astype(BF)
            return carry

        lax.fori_loop(0, images, image, 0, unroll=UNROLL)

        def keep(r):
            wout[r * hw : (r + 1) * hw, :] = w_ref[0, 3]
            o_all[r * hw : (r + 1) * hw, :] = o_ref[0]

        at_step(step, count, keep)

        @pl.when(step == count - 1)
        def _():
            finish(lambda at: dot_tn(o_all[:, at], wout[...]), (own_ref, peer_ref), starts, seq)

    def block_of(step, lens, place):
        return (place[2] + ahead + step) % total

    def out(*dims):
        index = lambda *at: (block_of(*at),) + (0,) * len(dims)
        return (shape((total,) + dims, BF), (1,) + dims, index)

    index = (lambda *at: (block_of(*at), 0, 0, 0)) if carry else (lambda *at: (0, 0, 0, 0))
    return call(
        kernel,
        "attn_fwd",
        (count,),
        [(x, None, None) for x in both + (cos, sin, jnp.asarray(swap_matrix(2 * hw).T, BF))]
        + [(weights, (1,) + weights.shape[1:], index)]
        + [(x, None, None) for x in starts],
        [out(heads, HD, rows)] * 3 + [out(hw, rows)] + halves_out(half, width, last),
        scratch=[
            pltpu.VMEM((5 * hw, width), BF),
            pltpu.VMEM((count * hw, width), BF),
            pltpu.VMEM((5 * hw, rows), F32),
            pltpu.VMEM((count * hw, rows), BF),
        ],
        scalars=(lens, place),
        flops=2 * count * rows * width * 6 * hw + 8 * count * rows * heads * seq * 256,
        moved=20_000_000,
        exps=count * rows * heads * seq,
        deps=deps,
        carry=carry,
        dynamic=True,
    )


def attn_bwd(lens, both, weights, part_of, starts, cos, sin, q, k, v, heads, seq, deps=()):
    begin, end = part_of
    count, (half, width), hw = end - begin, both[0].shape, heads * HD
    last = end == weights.shape[0]
    rows = 2 * half
    images, given = rows // seq, len(starts)
    scale = HD ** (-0.5)

    def kernel(lens, own_in, peer_in, cos_ref, sin_ref, swap_ref, q_ref, k_ref, v_ref, w_ref, *refs):
        starts, refs = refs[:given], refs[given:]
        dqkv_ref, own_ref, peer_ref, w_all, do_all, d_all = refs
        step = pl.program_id(0)
        do_all[:, :half] = dot_nt(w_ref[0, 3], own_in[...])
        do_all[:, half:] = dot_nt(w_ref[0, 3], peer_in[...])

        def image(i, carry):
            at = pl.ds(pl.multiple_of(i * seq, seq), seq)
            cos, sin = cos_ref[:, at], sin_ref[:, at]
            ok = lax.broadcasted_iota(jnp.int32, (seq, 1), 0) < lens[i]
            dqs, dks, dvs = [], [], []
            for h in range(heads):
                do = do_all[h * HD : (h + 1) * HD, at].astype(BF)
                q, k, v = q_ref[0, h, :, at], k_ref[0, h, :, at], v_ref[0, h, :, at]
                st = jnp.where(ok, dot_tn(k, q) * scale, NEG)
                dp = dot_tn(v, do)
                ex = jnp.exp(st - jnp.max(st, axis=0, keepdims=True))
                probs = ex * (1.0 / jnp.sum(ex, axis=0, keepdims=True))
                inner = jnp.sum(dp * probs, axis=0, keepdims=True)
                ds = (probs * (dp - inner)).astype(BF)
                dvs.append(dot_nt(do, probs.astype(BF)))
                dk = dot_nt(q, ds), dot_nt(dot(swap_ref[...], q).astype(BF), ds)
                dq = dot(k, ds), dot(dot(swap_ref[...], k).astype(BF), ds)
                dqs.append((dq[0] * cos - dq[1] * sin) * scale)
                dks.append((dk[0] * cos - dk[1] * sin) * scale)
            dqkv_ref[0, :, at] = jnp.concatenate(dqs + dks + dvs, axis=0).astype(BF)
            return carry

        lax.fori_loop(0, images, image, 0, unroll=UNROLL)

        def keep(r):
            for j in range(3):
                first = (r * 3 + j) * hw
                w_all[first : first + hw, :] = w_ref[0, j]
            d_all[r * 3 * hw : (r + 1) * 3 * hw, :] = dqkv_ref[0]

        at_step(step, count, keep)

        @pl.when(step == count - 1)
        def _():
            finish(lambda at: dot_tn(d_all[:, at], w_all[...]), (own_ref, peer_ref), starts, seq)

    return call(
        kernel,
        "attn_bwd",
        (count,),
        [(x, None, None) for x in both + (cos, sin, jnp.asarray(swap_matrix(HD).T, BF))]
        + [by_step(q), by_step(k), by_step(v), by_step(weights, begin)]
        + [(x, None, None) for x in starts],
        [step_out((count, 3 * hw, rows), BF)] + halves_out(half, width, last),
        scratch=[
            pltpu.VMEM((count * 3 * hw, width), BF),
            pltpu.VMEM((hw, rows), F32),
            pltpu.VMEM((count * 3 * hw, rows), BF),
        ],
        scalars=(lens,),
        flops=2 * count * rows * width * 4 * hw + 20 * count * rows * heads * seq * 256,
        moved=20_000_000,
        exps=count * rows * heads * seq,
        deps=deps,
    )


def tiles(refs, tile, body):
    half = refs[0].shape[0]
    for j, ref in enumerate(refs):
        for t in range(half // tile):
            body(ref, slice(t * tile, (t + 1) * tile), slice(j * half + t * tile, j * half + (t + 1) * tile))


def mlp_fwd(both, weights, deps=()):
    count, blocks, part, width = weights.shape
    rows, cols = 2 * both[0].shape[0], blocks * part
    units = cols // 2

    def kernel(own_in, peer_in, w_ref, gu_ref, hid_ref):
        weight = w_ref[0].reshape(cols, width)

        def block(ref, here, at):
            gu = dot_nt(ref[here, :], weight)
            gu_ref[0, at, :] = gu
            g, u = gu[:, :units], gu[:, units:]
            hid_ref[0, at, :] = (g * jax.nn.sigmoid(g) * u).astype(BF)

        tiles((own_in, peer_in), MLP_TILE, block)

    return call(
        kernel,
        "mlp_fwd",
        (count,),
        [(x, None, None) for x in both] + [by_step(weights)],
        [step_out((count, rows, cols), F32), step_out((count, rows, units), BF)],
        flops=2 * count * rows * width * cols,
        moved=26_000_000,
        exps=count * rows * units,
        deps=deps,
    )


def mlp_mid(both, downs, gate_up, deps=()):
    count, blocks, part, width = downs.shape
    rows, units = 2 * both[0].shape[0], blocks * part

    def kernel(own_in, peer_in, w_ref, gu_ref, dgu_ref):
        weight = w_ref[0].reshape(units, width)

        def block(ref, here, at):
            dhid = dot_nt(ref[here, :], weight)
            g, u = gu_ref[0, at, :units], gu_ref[0, at, units:]
            sig = jax.nn.sigmoid(g)
            dgu_ref[0, at, :units] = (dhid * u * sig * (1.0 + g * (1.0 - sig))).astype(BF)
            dgu_ref[0, at, units:] = (dhid * g * sig).astype(BF)

        tiles((own_in, peer_in), MLP_TILE, block)

    return call(
        kernel,
        "mlp_mid",
        (count,),
        [(x, None, None) for x in both] + [by_step(downs), by_step(gate_up)],
        [step_out((count, rows, 2 * units), BF)],
        flops=2 * count * rows * width * units,
        moved=26_000_000,
        exps=count * rows * units,
        deps=deps,
    )[0]


def back_out(values, weights, name, deps=()):
    count, rows, cols = values.shape
    width = weights.shape[3]
    tile = rows // 4

    def kernel(v_ref, w_ref, own_ref, peer_ref):
        t = pl.program_id(0)
        value = sum(dot(v_ref[r], w_ref[r].reshape(cols, width)) for r in range(count))

        @pl.when(t < 2)
        def _():
            own_ref[...] = value

        @pl.when(t >= 2)
        def _():
            peer_ref[...] = value.astype(BF)

    return call(
        kernel,
        name,
        (4,),
        [(values, (count, tile, cols), lambda t: (0, t, 0)), (weights, None, None)],
        [
            (shape((rows // 2, width), F32), (tile, width), lambda t: (jnp.minimum(t, 1), 0)),
            (shape((rows // 2, width), BF), (tile, width), lambda t: (jnp.maximum(t - 2, 0), 0)),
        ],
        flops=2 * count * rows * width * cols,
        moved=2 * values.size + 2 * weights.size + 3 * rows * width,
        deps=deps,
    )


ORDERS = {"x": ((1, 3), (0, 2)), "y": ((2, 3), (0, 1))}


def grad_split(place, pairs, parts, deps=()):
    half, width = pairs[0][0][0].shape
    rows, count = 2 * half, pairs[0][1].shape[0]
    last = [right.shape[2] == rows for _, right in pairs]
    widths = [right.shape[1 if flip else 2] for (_, right), flip in zip(pairs, last)]
    cols, strip, n = sum(widths), width // 8, len(pairs)

    def kernel(place, *refs):
        lefts, refs = refs[: 2 * n], refs[2 * n :]
        rights, refs = refs[:n], refs[n:]
        outs, refs = refs[: 2 * len(parts)], refs[2 * len(parts) :]
        turned, res = refs[:n], refs[n]

        @pl.when(pl.program_id(0) == 0)
        def _():
            for j, lt in enumerate(turned):
                lt[:, :half] = lefts[2 * j][...].T
                lt[:, half:] = lefts[2 * j + 1][...].T

        begin = 0
        for lt, right, size, flip in zip(turned, rights, widths, last):
            part = dot_nt(lt[...], right[0]) if flip else dot(lt[...], right[0])
            res[:, begin : begin + size] = part
            begin += size
        step = pl.program_id(0)
        for k, (begin, size, order, low, high) in enumerate(parts):

            @pl.when((step >= low) & (step < high))
            def _(k=k, begin=begin, size=size, order=order):
                for ref, blocks in zip(outs[2 * k : 2 * k + 2], ORDERS[order]):
                    for j, rel in enumerate(blocks):
                        for core in range(2):
                            first = ((place[0] ^ rel) * 2 + (place[1] ^ core)) * strip
                            rows_at = pl.ds(pl.multiple_of(first, 16), strip)
                            ref[j, 0, core] = res[rows_at, begin : begin + size].astype(BF)

    outs = []
    for _, size, _, low, high in parts:

        def index(z, low=low, high=high):
            return (0, jnp.clip(z, low, high - 1) - low, 0, 0, 0)

        out = (shape((2, high - low, 2, strip, size), BF), (2, 1, 2, strip, size), index)
        outs += [out, out]
    return call(
        kernel,
        "grad_split",
        (count,),
        [(x, None, None) for both, _ in pairs for x in both] + [by_step(right) for _, right in pairs],
        outs,
        scratch=[pltpu.VMEM((width, rows), BF)] * n + [pltpu.VMEM((width, cols), F32)],
        scalars=(place,),
        flops=2 * count * rows * width * cols,
        moved=2 * rows * width + 2 * count * rows * cols + 2 * count * width * cols,
        deps=deps,
    )


def assemble(place, base, chunks, deps=()):
    blocks, part, width = base.shape
    count = chunks[0][0].shape[0]

    def kernel(place, base, *refs):
        out = refs[-1]
        q = place[0]
        own = pl.program_id(0) == place[2]

        @pl.when(own)
        def _():
            out[0] = base[...]

        @pl.when(jnp.logical_not(own))
        def _():
            begin = 0
            for j in range(len(chunks)):
                near, fx, sy, fy, sx = refs[5 * j : 5 * j + 5]
                half, size = fx.shape[-2], near.shape[1]
                a, b = slice(begin, begin + half), slice(begin + half, begin + size)
                out[0, q, begin : begin + size] = near[0]
                out[0, q ^ 1, a] = fx[0, 0]
                out[0, q ^ 1, b] = sx[0, 0]
                out[0, q ^ 2, a] = fy[0, 0]
                out[0, q ^ 2, b] = sy[0, 0]
                out[0, q ^ 3, a] = fy[1, 0]
                out[0, q ^ 3, b] = sx[1, 0]
                begin += size

    def far(array, whole):
        def index(z, place):
            back = (place[2] + count - z) % count
            return (0 if whole else 1, jnp.maximum(back - 1, 0), 0, 0)

        return (array, (2 if whole else 1, 1) + array.shape[2:], index)

    ins = [(base, None, None)]
    for near, *others in chunks:
        ins += [(near, (1,) + near.shape[1:], lambda z, place: (z, 0, 0))] + [far(x, j > 1) for j, x in enumerate(others)]
    return call(
        kernel,
        "assemble",
        (count,),
        ins,
        [(shape((count,) + base.shape, BF), (1,) + base.shape, lambda z, place: (z, 0, 0, 0))],
        scalars=(place,),
        moved=4 * count * base.size,
        deps=deps,
        dynamic=True,
    )[0]


def norm(x):
    centered = x - jnp.mean(x, axis=-1, keepdims=True)
    inverse = lax.rsqrt(jnp.mean(centered * centered, axis=-1, keepdims=True) + EPSILON)
    return centered * inverse, inverse


def norm_back(d_normed, normed, inverse, scale):
    d_hat = d_normed * (1.0 + scale)
    return inverse * (
        d_hat
        - jnp.mean(d_hat, axis=-1, keepdims=True)
        - normed * jnp.mean(d_hat * normed, axis=-1, keepdims=True)
    )


def total(x):
    return jnp.sum(x, axis=0, keepdims=True)


SHIFT_ONE, SCALE_ONE, GATE_ONE, SHIFT_TWO, SCALE_TWO, GATE_TWO = range(6)


def by_image(body, name, lengths, mod, rows_in, bias, outs, sums, deps=()):
    images, _, width = mod.shape
    seq = rows_in[0].shape[0] // images
    count = len(rows_in)

    def kernel(lens, mod_ref, bias_ref, *refs):
        row_id = lax.broadcasted_iota(jnp.int32, (seq, 1), 0)
        mask = jnp.where(row_id < lens[pl.program_id(0)], 1.0, 0.0).astype(F32)
        values = [ref[...].astype(F32) for ref in refs[:count]]
        got = body(mask, [mod_ref[0, j : j + 1, :] for j in range(6)], bias_ref[...], *values)
        for ref, value in zip(refs[count:-1], got):
            ref[...] = value.astype(ref.dtype)
        for j, value in enumerate(got[len(outs) :]):
            refs[-1][0, j : j + 1, :] = value

    block = ((seq, width), lambda i: (i, 0))
    return call(
        kernel,
        name,
        (images,),
        [(mod, (1, 6, width), lambda i: (i, 0, 0)), (bias, None, None)]
        + [(x,) + block for x in rows_in],
        [(shape(rows_in[0].shape, dtype),) + block for dtype in outs]
        + [(shape((images, sums, width), F32), (1, sums, width), lambda i: (i, 0, 0))],
        scalars=(lengths,),
        flops=1,
        moved=1,
        deps=deps,
    )


def pre_attention(mask, mod, bias, x, upstream):
    normed, _ = norm(x)
    dm = mask * mod[GATE_TWO] * upstream
    return normed * (1.0 + mod[SCALE_ONE]) + mod[SHIFT_ONE], dm, total(dm), total(mask * x * x)


def pre_mlp(mask, mod, bias, x, att_own, att_peer):
    gated = mask * mod[GATE_ONE] * (att_own + att_peer + bias)
    residual = x + gated
    normed, _ = norm(residual)
    return residual, normed * (1.0 + mod[SCALE_TWO]) + mod[SHIFT_TWO], total(gated * gated)


def post_mlp(mask, mod, bias, residual, upstream, mlp_own, mlp_peer):
    branch = mlp_own + mlp_peer + bias
    gated = mask * mod[GATE_TWO] * branch
    return residual + gated, total(mask * branch * upstream), total(gated * gated)


def back_mlp(mask, mod, bias, residual, upstream, att_own, att_peer, da_own, da_peer):
    normed, inverse = norm(residual)
    da = da_own + da_peer
    dh = upstream + norm_back(da, normed, inverse, mod[SCALE_TWO])
    d_att = mask * mod[GATE_ONE] * dh
    branch = att_own + att_peer + bias
    return dh, d_att, total(mask * branch * dh), total(da), total(da * normed), total(d_att)


def back_attention(mask, mod, bias, x, dh, da_own, da_peer):
    normed, inverse = norm(x)
    da = da_own + da_peer
    return dh + norm_back(da, normed, inverse, mod[SCALE_ONE]), total(da), total(da * normed)


def ring(count, shift):
    return [(i, (i + shift) % count) for i in range(count)]


def take(array, index, axis):
    return lax.dynamic_index_in_dim(array, index, axis, keepdims=False)


def local(
    sizes,
    patches,
    conditioning,
    time_bins,
    lengths,
    positions,
    time_table,
    w_ada,
    b_ada,
    w_qkv,
    w_out,
    branch_bias,
    w_gu,
    w_down,
    d_out,
):
    axes = tuple(sizes)
    ny, nx, nc, tn = sizes.values()
    square = nx == 2 and ny == 2
    at_y, at_x, at_c, at_z = (lax.axis_index(name) for name in axes)
    at_q = at_y * nx + at_x
    devices = ny * nx * nc * tn
    image_count, width = conditioning.shape
    rows = patches.shape[0]
    seq = rows // image_count
    heads = w_qkv.shape[2] // HD // nc
    hw = heads * HD
    units = w_gu.shape[2] // nc
    strip = width // (ny * nx * nc)
    place = jnp.stack([at_q, at_c, at_z]).astype(jnp.int32)
    swap = ring(2, 1)

    def peer(value):
        return lax.ppermute(value, "c", ring(nc, 1))

    def core_share(weight, axis):
        size = weight.shape[axis] // nc
        return lax.dynamic_slice_in_dim(weight, at_c * size, size, axis)

    def later(values, marks):
        return lax.optimization_barrier((values, marks))[0] if marks else values

    def along_z(piece):
        return lax.all_to_all(jnp.broadcast_to(piece[None], (tn,) + piece.shape), "z", 0, 0)

    def plane_parts(near):
        half = (near.shape[1] // 2 + 15) // 16 * 16
        others = [take(near, (at_z + tn - r) % tn, 0) for r in range(1, tn)]
        return jnp.stack([x[:half] for x in others]), jnp.stack([x[half:] for x in others])

    def plane_first(parts, *marks):
        first, second = parts
        first_x = lax.ppermute(first, "x", swap)
        second_y = lax.ppermute(second, "y", swap)
        first_x, second_y = later((first_x, second_y), marks)
        return jnp.stack([first, first_x]), jnp.stack([second, second_y])

    def plane_second(pairs, *marks):
        crossed = lax.ppermute(pairs[0], "y", swap), lax.ppermute(pairs[1], "x", swap)
        return later(crossed, marks)

    def chunk(near, pairs, crossed):
        return near, pairs[0], pairs[1], crossed[0], crossed[1]

    def plane_plain(near, base):
        whole = lax.all_gather(near, ("y", "x"), axis=1)
        return whole.reshape((tn,) + base.shape)

    qkv_t = w_qkv.transpose(1, 2, 0)
    if square:
        heads_piece = jnp.where(
            at_q < 3,
            lax.dynamic_slice(qkv_t, (jnp.minimum(at_q, 2), at_c * hw, 0), (1, hw, width))[0],
            core_share(w_out, 0),
        )
    heads_own = jnp.concatenate([core_share(qkv_t, 1), core_share(w_out, 0)[None]], axis=0)
    gu_own = core_share(w_gu.transpose(1, 2, 0), 1).reshape(4, units // 2, width)
    down_own = core_share(w_down, 0).reshape(4, units // 4, width)
    if square:
        near_heads = along_z(heads_piece)
    else:
        flat = lambda own: take(own.reshape(ny * nx, -1, width), at_q, 0)
        heads_all, gu_all, down_all = (
            plane_plain(along_z(flat(own)), own) for own in (heads_own, gu_own, down_own)
        )

    def reduce_first(pairs, parts, deps=()):
        outs = grad_split(place, pairs, parts, deps)
        sent, kept = tuple(outs[::2]), tuple(outs[1::2])
        got = tuple(lax.ppermute(x, part[2], swap) for x, part in zip(sent, parts))
        return (kept, got), sent

    def reduce_send(state, *marks):
        kept, got = later(state, marks)
        return tuple((k[1].astype(F32) + g[1].astype(F32)).astype(BF) for k, g in zip(kept, got))

    def reduce_second(state, sends, parts, *marks):
        other = {"x": "y", "y": "x"}
        got = tuple(lax.ppermute(x, other[part[2]], swap) for x, part in zip(sends, parts))
        got = later(got, marks)
        return tuple(
            (k[0].astype(F32) + g[0].astype(F32) + h.astype(F32)).astype(BF)
            for k, g, h in zip(*state, got)
        )

    def reduce_plain(pairs):
        flip = lambda right: right.swapaxes(1, 2) if right.shape[2] == 2 * rows else right
        full = jnp.concatenate(
            [
                jnp.einsum(
                    "rd,zrn->zdn", jnp.concatenate(both), flip(right), preferred_element_type=F32
                )
                for both, right in pairs
            ],
            axis=2,
        )
        full = full.astype(BF).reshape(full.shape[0], ny * nx, nc, strip, -1)
        summed = lax.psum_scatter(full, ("y", "x"), scatter_dimension=1, tiled=False)
        return jnp.stack([take(summed, at_c, 1), take(summed, 1 - at_c, 1)], axis=1)

    def reduce_z(rows, *marks):
        return later(lax.all_to_all(rows, "z", 0, 0), marks)

    def reduce_z_steps(rows, *marks):
        got = [take(rows, at_z, 0)]
        for r in range(1, tn):
            sent = take(rows, (at_z + tn - r) % tn, 0)
            got.append(lax.ppermute(sent, "z", ring(tn, -r)))
        return jnp.stack(later(got, marks))

    def reduce_core(arrived):
        summed = jnp.sum(arrived.astype(F32), axis=0)
        own, got = summed[0], peer(summed[1].astype(BF)).astype(F32)
        first = at_c == 0
        return jnp.stack([jnp.where(first, own, got), jnp.where(first, got, own)])

    bins = jnp.arange(time_table.shape[0], dtype=jnp.int32)
    onehot = (time_bins[:, None] == bins[None, :]).astype(F32)
    cond_vec = conditioning + jnp.dot(onehot, time_table, precision=EXACT)
    cond_sig = jax.nn.sigmoid(cond_vec)
    silu_low = (cond_vec * cond_sig).astype(BF)
    mod = (dot(silu_low, w_ada) + b_ada).reshape(image_count, 6, width)
    bias_attn, bias_mlp = branch_bias[None, :width], branch_bias[None, width:]
    elementwise = functools.partial(by_image, lengths=lengths, mod=mod)
    a1_own, dm_own, sums_pre = elementwise(
        pre_attention, "pre_attention", rows_in=(patches, d_out), bias=bias_attn, outs=(BF, BF), sums=2
    )
    a1_all = (a1_own, peer(a1_own))
    facts = jnp.concatenate([positions.reshape(-1), lengths])
    facts_peer = peer(facts)
    lens = jnp.concatenate([lengths, facts_peer[2 * rows :]])
    pos = jnp.concatenate([positions, facts_peer[: 2 * rows].reshape(2, rows)], axis=1).astype(F32)
    quarter = HD // 4
    frequency = 10000.0 ** (-jnp.arange(quarter, dtype=F32) / quarter)
    angle = pos[:, None, :] * frequency[None, :, None]
    cosine, sine = jnp.cos(angle), jnp.sin(angle)
    cos = jnp.concatenate([cosine[0], cosine[0], cosine[1], cosine[1]], axis=0)
    sin = jnp.concatenate([sine[0], sine[0], sine[1], sine[1]], axis=0)
    def spread(value):
        return lax.all_to_all(jnp.broadcast_to(value[None], (devices,) + value.shape), axes, 0, 0)

    early = jnp.concatenate([silu_low.astype(F32), time_bins[:, None].astype(F32)], axis=1)
    own_heads = attn_fwd(
        lens, place, a1_all, heads_own[None], 1, tn, (), (), cos, sin, heads, seq
    )

    def attend(deps):
        return attn_fwd(
            lens, place, a1_all, heads_all, tn - 1, tn, tuple(own_heads[:4]), own_heads[4:],
            cos, sin, heads, seq, deps=deps,
        )

    def into_mlp(deps):
        return elementwise(
            pre_mlp,
            "pre_mlp",
            rows_in=(patches,) + att,
            bias=bias_attn,
            outs=(F32, BF),
            sums=1,
            deps=deps,
        )

    if square:
        gu_piece, near_heads = later((take(gu_own, at_q, 0), near_heads), (a1_own,))
        near_gu = along_z(gu_piece)
        pairs_heads = plane_first(plane_parts(near_heads))
        crossed_heads = plane_second(pairs_heads, own_heads[4])
        near_gu = later(near_gu, (crossed_heads,))
        parts_gu = plane_parts(near_gu)
        down_piece = later(take(down_own, at_q, 0), (near_gu,))
        near_down = along_z(down_piece)
        heads_all = assemble(
            place, heads_own, [chunk(near_heads, pairs_heads, crossed_heads)], deps=parts_gu
        )
        pairs_gu = plane_first(parts_gu, heads_all)
        q, k, v, attended, att_own, att_peer = attend(pairs_gu)
        crossed_gu = plane_second(pairs_gu, att_own)
        near_down = later(near_down, (att_own,))
        parts_down = plane_parts(near_down)
        att = (att_own, peer(att_peer))
        early = later(early, (near_down,))
        residual, a2_own, sums_att = into_mlp(crossed_gu + parts_down)
        pairs_down = plane_first(parts_down, a2_own)
        gu_all = assemble(place, gu_own, [chunk(near_gu, pairs_gu, crossed_gu)], deps=(a2_own,))
        early_all = spread(early)
        wait_mlp = pairs_down + (early_all,)
    else:
        q, k, v, attended, att_own, att_peer = attend(())
        att = (att_own, peer(att_peer))
        residual, a2_own, sums_att = into_mlp(())
        wait_mlp = ()
        early_all = spread(early)
    a2_all = (a2_own, peer(a2_own))
    dm_all = (dm_own, peer(dm_own))
    gate_up, hidden = mlp_fwd(a2_all, gu_all, deps=wait_mlp)

    def finish_mlp(deps):
        return elementwise(
            post_mlp,
            "post_mlp",
            rows_in=(residual, d_out, mlp_own, peer(mlp_peer)),
            bias=bias_mlp,
            outs=(F32,),
            sums=2,
            deps=deps,
        )

    def through_mlp(deps):
        return elementwise(
            back_mlp,
            "back_mlp",
            rows_in=(residual, d_out) + att + (da2_own, peer(da2_peer)),
            bias=bias_attn,
            outs=(F32, BF),
            sums=4,
            deps=deps,
        )

    def back_heads(deps):
        return attn_bwd(
            lens, da_all, heads_all, (0, tn), (), cos, sin, q, k, v, heads, seq, deps=deps
        )

    def through_attention(deps):
        return elementwise(
            back_attention,
            "back_attention",
            rows_in=(patches, dh, da1_own, peer(da1_peer)),
            bias=bias_attn,
            outs=(F32,),
            sums=2,
            deps=deps,
        )

    if square:
        crossed_down = plane_second(pairs_down, hidden)
        mid = tn // 2
        down_parts = ((0, units, "x", 0, tn),)
        gu_parts = (
            (0, units, "x", 0, mid),
            (units, units, "y", 0, mid),
            (0, units, "x", mid, tn),
            (units, units, "y", mid, tn),
        )
        rest = 4 * hw - 512
        heads_parts = (
            (0, 256, "x", 0, tn),
            (256, 256, "y", 0, tn),
            (512, rest, "x", 0, mid),
            (512, rest, "y", mid, tn),
        )
        down_state, down_sent = reduce_first([(dm_all, hidden)], down_parts, crossed_down)
        down_all = assemble(
            place, down_own, [chunk(near_down, pairs_down, crossed_down)], deps=down_sent
        )
        d_gate_up = mlp_mid(dm_all, down_all, gate_up, deps=down_sent)
        gu_state, gu_sent = reduce_first([(a2_all, d_gate_up)], gu_parts)
        one, two = ((gu_state[0][k : k + 2], gu_state[1][k : k + 2]) for k in (0, 2))
        down_sends = reduce_send(down_state, gu_sent)
        da2_own, da2_peer = back_out(d_gate_up, gu_all, "mlp_back", deps=gu_sent + down_sends)
        one_sends = reduce_send(one, da2_own)
        dh, da_own, sums_back = through_mlp(one_sends)
        da_all = (da_own, peer(da_own))
        two_sends = reduce_send(two, da_own)
        one_rows = reduce_second(one, one_sends, gu_parts[:2], da_own)
        d_qkv, da1_own, da1_peer = back_heads(down_sends + two_sends + one_rows)
        down_rows = reduce_second(down_state, down_sends, down_parts, d_qkv)
        two_rows = reduce_second(two, two_sends, gu_parts[2:], d_qkv)
        gu_rows = jnp.concatenate(
            [jnp.concatenate(half, axis=3) for half in (one_rows, two_rows)], axis=0
        )
        mlp_rows = jnp.concatenate([gu_rows, down_rows[0]], axis=3)
        heads_state, heads_sent = reduce_first(
            [(a1_all, d_qkv), (da_all, attended)], heads_parts, (mlp_rows,)
        )
        d_inputs, sums_one = through_attention(heads_sent)
        mlp_own, mlp_peer = back_out(hidden, down_all, "mlp_out", deps=(sums_one,))
        mlp_z = reduce_z(mlp_rows, mlp_own)
        heads_sends = reduce_send(heads_state, mlp_own)
        output, sums_mlp = finish_mlp(heads_sends)
        heads_rows = reduce_second(heads_state, heads_sends, heads_parts, sums_mlp)
        heads_rows = jnp.concatenate(
            heads_rows[:2] + (jnp.concatenate(heads_rows[2:], axis=0),), axis=3
        )
        grad_mlp = reduce_core(mlp_z)
        grad_gu, grad_down = grad_mlp[:, :, : 2 * units], grad_mlp[:, :, 2 * units :]
    else:
        d_gate_up = mlp_mid(dm_all, down_all, gate_up)
        da2_own, da2_peer = back_out(d_gate_up, gu_all, "mlp_back")
        dh, da_own, sums_back = through_mlp(())
        da_all = (da_own, peer(da_own))
        mlp_own, mlp_peer = back_out(hidden, down_all, "mlp_out")
        output, sums_mlp = finish_mlp(())
        d_qkv, da1_own, da1_peer = back_heads(())
        d_inputs, sums_one = through_attention(())
        grad_down, grad_gu, grad_heads = (
            reduce_core(reduce_z(reduce_plain(pairs)))
            for pairs in (
                [(dm_all, hidden)],
                [(a2_all, d_gate_up)],
                [(a1_all, d_qkv), (da_all, attended)],
            )
        )

    d_mod = jnp.concatenate([sums_one, sums_back[:, :3], sums_mlp[:, :1]], axis=1)
    d_mod = d_mod.reshape(image_count, 6 * width)
    d_bias = jnp.concatenate([jnp.sum(sums_back[:, 3], axis=0), jnp.sum(sums_pre[:, 0], axis=0)])
    sums = jnp.stack(
        [
            jnp.sum(sums_pre[:, 1]),
            jnp.sum(sums_att),
            jnp.sum(sums_mlp[:, 1]),
            jnp.sum(lengths).astype(F32),
        ]
    )
    ada_cols, bias_cols = 6 * width // devices, 2 * width // devices
    ready = jnp.concatenate(
        [
            d_mod.reshape(image_count, devices, ada_cols).transpose(1, 0, 2).reshape(devices, -1),
            d_bias.reshape(devices, bias_cols),
            jnp.broadcast_to(sums[None], (devices, 4)),
        ],
        axis=1,
    )
    if square:
        ready, mlp_z = lax.optimization_barrier((ready, mlp_z))
    arrived = lax.all_to_all(ready, axes, 0, 0, tiled=True)
    if square:
        d_mod, heads_rows = lax.optimization_barrier((d_mod, heads_rows))
    d_silu = dot_nt(d_mod.astype(BF), w_ada)
    d_cond = d_silu * cond_sig * (1.0 + cond_vec * (1.0 - cond_sig))
    if square:
        arrived, d_cond = lax.optimization_barrier((arrived, d_cond))
    d_cond_all = spread(d_cond).reshape(devices * image_count, width)
    if square:
        grad_heads = reduce_core(reduce_z_steps(heads_rows, d_cond_all))
    ends = np.cumsum([0, image_count * ada_cols, bias_cols, 4])
    d_mod_all, bias_all, sums_all = (
        arrived[:, start:stop] for start, stop in zip(ends[:-1], ends[1:])
    )
    d_mod_all = d_mod_all.reshape(devices * image_count, ada_cols)
    grad_b_ada = jnp.sum(d_mod_all, axis=0)
    grad_bias = jnp.sum(bias_all, axis=0)
    sums_all = jnp.sum(sums_all, axis=0)
    rms_values = jnp.sqrt(sums_all[:3] / (sums_all[3] * width))
    early_all = early_all.reshape(devices * image_count, -1)
    silu_all, bins_all = early_all[:, :width].astype(BF), early_all[:, width].astype(jnp.int32)
    grad_ada = dot_tn(silu_all, d_mod_all.astype(BF))
    table_rows = time_table.shape[0] // devices
    flat = (at_q * nc + at_c) * tn + at_z
    own_bins = flat * table_rows + jnp.arange(table_rows, dtype=jnp.int32)
    picks = (own_bins[:, None] == bins_all[None, :]).astype(F32)
    grad_table = jnp.dot(picks, d_cond_all, precision=EXACT)

    def joined(value, parts):
        both = [value[j].reshape(strip, parts, -1) for j in range(nc)]
        return jnp.concatenate(both, axis=2)

    return (
        output,
        d_inputs,
        d_cond,
        joined(grad_heads[:, :, : 3 * hw], 3),
        joined(grad_heads[:, :, 3 * hw :], 1)[:, 0].T,
        joined(grad_gu, 2),
        joined(grad_down, 1)[:, 0].T,
        grad_ada,
        grad_b_ada,
        grad_bias,
        grad_table,
        rms_values,
    )


def solution(mesh):
    groups, tn = mesh.shape["dp"], mesh.shape["tensor"]
    nc, nx = 2, 2
    sizes = {"y": groups // (nx * nc), "x": nx, "c": nc, "z": tn}
    fine = Mesh(mesh.devices.reshape(tuple(sizes.values())), tuple(sizes))
    dp = ("y", "x", "c")
    every = dp + ("z",)
    return jax.shard_map(
        functools.partial(local, sizes),
        mesh=fine,
        in_specs=(
            P(every, None),
            P(every, None),
            P(every),
            P(every),
            P(None, every),
            P(),
            P(),
            P(),
            P(None, None, "z"),
            P("z", None),
            P(),
            P(None, None, "z"),
            P("z", None),
            P(every, None),
        ),
        out_specs=(
            P(every, None),
            P(every, None),
            P(every, None),
            P(dp, None, "z"),
            P("z", dp),
            P(dp, None, "z"),
            P("z", dp),
            P(None, every),
            P(every),
            P(every),
            P(every, None),
            P(),
        ),
        check_vma=False,
    )
```

```python
import functools

import jax
import jax.numpy as jnp
import numpy as np
from jax import lax
from jax.experimental import pallas as pl
from jax.experimental.pallas import tpu as pltpu
from jax.sharding import Mesh
from jax.sharding import PartitionSpec as P

HD = 72
EXACT = lax.Precision.HIGHEST
EPSILON = 1e-06
NEG = -1e30
VMEM_LIMIT = 58 * 1024 * 1024
UNROLL = 4
MLP_TILE = 256
BF = jnp.bfloat16
F32 = jnp.float32
NT = (((1,), (1,)), ((), ()))
TN = (((0,), (0,)), ((), ()))


def dot(a, b):
    return jnp.dot(a, b, preferred_element_type=F32)


def dot_nt(a, b):
    return lax.dot_general(a, b, NT, preferred_element_type=F32)


def dot_tn(a, b):
    return lax.dot_general(a, b, TN, preferred_element_type=F32)


def call(kernel, name, grid, ins, outs, scratch=(), scalars=(), flops=0, moved=0, exps=0, deps=(), carry=(), dynamic=False):
    def spec(shape, block, index):
        if block is None:
            return pl.BlockSpec(shape, lambda *_: (0,) * len(shape))
        return pl.BlockSpec(block, index if dynamic else lambda *at: index(*at[: len(grid)]))

    arrays = [item[0] for item in ins]
    in_specs = [spec(item[0].shape, item[1], item[2]) for item in ins]
    out_specs = [spec(item[0].shape, item[1], item[2]) for item in outs]
    count_s, count_i, count_d = len(scalars), len(ins), len(deps) + len(carry)

    def body(*refs):
        kept = refs[: count_s + count_i] + refs[count_s + count_i + count_d :]
        kernel(*kept)

    return pl.pallas_call(
        body,
        grid_spec=pltpu.PrefetchScalarGridSpec(
            num_scalar_prefetch=count_s,
            grid=grid,
            in_specs=in_specs + [pl.BlockSpec(memory_space=pl.ANY)] * count_d,
            out_specs=out_specs,
            scratch_shapes=list(scratch),
        ),
        out_shape=[item[0] for item in outs],
        compiler_params=pltpu.CompilerParams(
            dimension_semantics=("arbitrary",) * len(grid), vmem_limit_bytes=VMEM_LIMIT
        ),
        cost_estimate=pl.CostEstimate(flops=flops, bytes_accessed=moved, transcendentals=exps),
        input_output_aliases={count_s + count_i + len(deps) + j: j for j in range(len(carry))},
        name=name,
    )(*scalars, *arrays, *deps, *carry)


def shape(dims, dtype):
    return jax.ShapeDtypeStruct(tuple(dims), dtype)


def swap_matrix(width):
    quarter = HD // 4
    out = np.zeros((width, width), np.float32)
    for lane in range(width):
        if (lane % HD) % (2 * quarter) < quarter:
            out[lane + quarter, lane] = -1.0
        else:
            out[lane - quarter, lane] = 1.0
    return out


def head_mask(heads, which, dtype):
    lane = lax.broadcasted_iota(jnp.int32, (1, heads * HD), 1)
    inside = (lane >= which * HD) & (lane < (which + 1) * HD)
    return jnp.where(inside, 1.0, 0.0).astype(F32).astype(dtype)


def finish(parts, outs, starts, tile):
    half = outs[0].shape[0]
    for j, ref in enumerate(outs):
        for t in range(half // tile):
            at = slice(t * tile, (t + 1) * tile)
            value = parts(slice(j * half + t * tile, j * half + (t + 1) * tile))
            if starts:
                value = value + starts[j][at, :]
            ref[at, :] = value.astype(ref.dtype)


def add_into(step, acc, rows, part):
    @pl.when(step == 0)
    def _():
        acc[rows, :] = part

    @pl.when(step > 0)
    def _():
        acc[rows, :] = acc[rows, :] + part


def at_step(step, count, body):
    for r in range(count):

        @pl.when(step == r)
        def _(r=r):
            body(r)


def halves_out(rows, width, last):
    return [(shape((rows, width), F32), None, None), (shape((rows, width), BF if last else F32), None, None)]


def by_step(array, begin=0):
    return (array, (1,) + array.shape[1:], lambda z: (z + begin,) + (0,) * (array.ndim - 1))


def step_out(dims, dtype):
    return (shape(dims, dtype), (1,) + tuple(dims[1:]), lambda z: (z,) + (0,) * (len(dims) - 1))


def attn_fwd(lens, place, both, weights, count, total, carry, starts, cos, sin, heads, seq, deps=()):
    (half, width), hw = both[0].shape, heads * HD
    ahead = 1 if carry else 0
    last = bool(carry)
    rows = 2 * half
    images, given = rows // seq, len(starts)
    scale = HD ** (-0.5)

    def kernel(lens, place, own_in, peer_in, cos_ref, sin_ref, swap_ref, w_ref, *refs):
        starts, refs = refs[:given], refs[given:]
        q_ref, k_ref, v_ref, o_ref, own_ref, peer_ref, wcat, wout, full, o_all = refs
        step = pl.program_id(0)
        for j in range(3):
            wcat[j * hw : (j + 1) * hw, :] = w_ref[0, j]
        wcat[3 * hw :, :] = dot(swap_ref[...], wcat[: 2 * hw, :]).astype(BF)
        full[:, :half] = dot_nt(wcat[...], own_in[...])
        full[:, half:] = dot_nt(wcat[...], peer_in[...])

        def image(i, carry):
            at = pl.ds(pl.multiple_of(i * seq, seq), seq)
            cos, sin = cos_ref[:, at], sin_ref[:, at]
            ok = lax.broadcasted_iota(jnp.int32, (seq, 1), 0) < lens[i]
            outs = []
            for h in range(heads):
                part = lambda j: full[j * hw + h * HD : j * hw + (h + 1) * HD, at]
                q = (part(0) * cos + part(3) * sin).astype(BF)
                k = (part(1) * cos + part(4) * sin).astype(BF)
                v = part(2).astype(BF)
                q_ref[0, h, :, at] = q
                k_ref[0, h, :, at] = k
                v_ref[0, h, :, at] = v
                st = jnp.where(ok, dot_tn(k, q) * scale, NEG)
                ex = jnp.exp(st - jnp.max(st, axis=0, keepdims=True))
                probs = (ex * (1.0 / jnp.sum(ex, axis=0, keepdims=True))).astype(BF)
                outs.append(dot(v, probs))
            o_ref[0, :, at] = jnp.concatenate(outs, axis=0).astype(BF)
            return carry

        lax.fori_loop(0, images, image, 0, unroll=UNROLL)

        def keep(r):
            wout[r * hw : (r + 1) * hw, :] = w_ref[0, 3]
            o_all[r * hw : (r + 1) * hw, :] = o_ref[0]

        at_step(step, count, keep)

        @pl.when(step == count - 1)
        def _():
            finish(lambda at: dot_tn(o_all[:, at], wout[...]), (own_ref, peer_ref), starts, seq)

    def block_of(step, lens, place):
        return (place[2] + ahead + step) % total

    def out(*dims):
        index = lambda *at: (block_of(*at),) + (0,) * len(dims)
        return (shape((total,) + dims, BF), (1,) + dims, index)

    index = (lambda *at: (block_of(*at), 0, 0, 0)) if carry else (lambda *at: (0, 0, 0, 0))
    return call(
        kernel,
        "attn_fwd",
        (count,),
        [(x, None, None) for x in both + (cos, sin, jnp.asarray(swap_matrix(2 * hw).T, BF))]
        + [(weights, (1,) + weights.shape[1:], index)]
        + [(x, None, None) for x in starts],
        [out(heads, HD, rows)] * 3 + [out(hw, rows)] + halves_out(half, width, last),
        scratch=[
            pltpu.VMEM((5 * hw, width), BF),
            pltpu.VMEM((count * hw, width), BF),
            pltpu.VMEM((5 * hw, rows), F32),
            pltpu.VMEM((count * hw, rows), BF),
        ],
        scalars=(lens, place),
        flops=2 * count * rows * width * 6 * hw + 8 * count * rows * heads * seq * 256,
        moved=20_000_000,
        exps=count * rows * heads * seq,
        deps=deps,
        carry=carry,
        dynamic=True,
    )


def attn_bwd(lens, both, weights, part_of, starts, cos, sin, q, k, v, heads, seq, deps=()):
    begin, end = part_of
    count, (half, width), hw = end - begin, both[0].shape, heads * HD
    last = end == weights.shape[0]
    rows = 2 * half
    images, given = rows // seq, len(starts)
    scale = HD ** (-0.5)

    def kernel(lens, own_in, peer_in, cos_ref, sin_ref, swap_ref, q_ref, k_ref, v_ref, w_ref, *refs):
        starts, refs = refs[:given], refs[given:]
        dqkv_ref, own_ref, peer_ref, w_all, do_all, d_all = refs
        step = pl.program_id(0)
        do_all[:, :half] = dot_nt(w_ref[0, 3], own_in[...])
        do_all[:, half:] = dot_nt(w_ref[0, 3], peer_in[...])

        def image(i, carry):
            at = pl.ds(pl.multiple_of(i * seq, seq), seq)
            cos, sin = cos_ref[:, at], sin_ref[:, at]
            ok = lax.broadcasted_iota(jnp.int32, (seq, 1), 0) < lens[i]
            dqs, dks, dvs = [], [], []
            for h in range(heads):
                do = do_all[h * HD : (h + 1) * HD, at].astype(BF)
                q, k, v = q_ref[0, h, :, at], k_ref[0, h, :, at], v_ref[0, h, :, at]
                st = jnp.where(ok, dot_tn(k, q) * scale, NEG)
                dp = dot_tn(v, do)
                ex = jnp.exp(st - jnp.max(st, axis=0, keepdims=True))
                probs = ex * (1.0 / jnp.sum(ex, axis=0, keepdims=True))
                inner = jnp.sum(dp * probs, axis=0, keepdims=True)
                ds = (probs * (dp - inner)).astype(BF)
                dvs.append(dot_nt(do, probs.astype(BF)))
                dk = dot_nt(q, ds), dot_nt(dot(swap_ref[...], q).astype(BF), ds)
                dq = dot(k, ds), dot(dot(swap_ref[...], k).astype(BF), ds)
                dqs.append((dq[0] * cos - dq[1] * sin) * scale)
                dks.append((dk[0] * cos - dk[1] * sin) * scale)
            dqkv_ref[0, :, at] = jnp.concatenate(dqs + dks + dvs, axis=0).astype(BF)
            return carry

        lax.fori_loop(0, images, image, 0, unroll=UNROLL)

        def keep(r):
            for j in range(3):
                first = (r * 3 + j) * hw
                w_all[first : first + hw, :] = w_ref[0, j]
            d_all[r * 3 * hw : (r + 1) * 3 * hw, :] = dqkv_ref[0]

        at_step(step, count, keep)

        @pl.when(step == count - 1)
        def _():
            finish(lambda at: dot_tn(d_all[:, at], w_all[...]), (own_ref, peer_ref), starts, seq)

    return call(
        kernel,
        "attn_bwd",
        (count,),
        [(x, None, None) for x in both + (cos, sin, jnp.asarray(swap_matrix(HD).T, BF))]
        + [by_step(q), by_step(k), by_step(v), by_step(weights, begin)]
        + [(x, None, None) for x in starts],
        [step_out((count, 3 * hw, rows), BF)] + halves_out(half, width, last),
        scratch=[
            pltpu.VMEM((count * 3 * hw, width), BF),
            pltpu.VMEM((hw, rows), F32),
            pltpu.VMEM((count * 3 * hw, rows), BF),
        ],
        scalars=(lens,),
        flops=2 * count * rows * width * 4 * hw + 20 * count * rows * heads * seq * 256,
        moved=20_000_000,
        exps=count * rows * heads * seq,
        deps=deps,
    )


def tiles(refs, tile, body):
    half = refs[0].shape[0]
    for j, ref in enumerate(refs):
        for t in range(half // tile):
            body(ref, slice(t * tile, (t + 1) * tile), slice(j * half + t * tile, j * half + (t + 1) * tile))


def mlp_fwd(both, weights, deps=()):
    count, blocks, part, width = weights.shape
    rows, cols = 2 * both[0].shape[0], blocks * part
    units = cols // 2

    def kernel(own_in, peer_in, w_ref, gu_ref, hid_ref):
        weight = w_ref[0].reshape(cols, width)

        def block(ref, here, at):
            gu = dot_nt(ref[here, :], weight)
            gu_ref[0, at, :] = gu
            g, u = gu[:, :units], gu[:, units:]
            hid_ref[0, at, :] = (g * jax.nn.sigmoid(g) * u).astype(BF)

        tiles((own_in, peer_in), MLP_TILE, block)

    return call(
        kernel,
        "mlp_fwd",
        (count,),
        [(x, None, None) for x in both] + [by_step(weights)],
        [step_out((count, rows, cols), F32), step_out((count, rows, units), BF)],
        flops=2 * count * rows * width * cols,
        moved=26_000_000,
        exps=count * rows * units,
        deps=deps,
    )


def mlp_mid(both, downs, gate_up, deps=()):
    count, blocks, part, width = downs.shape
    rows, units = 2 * both[0].shape[0], blocks * part

    def kernel(own_in, peer_in, w_ref, gu_ref, dgu_ref):
        weight = w_ref[0].reshape(units, width)

        def block(ref, here, at):
            dhid = dot_nt(ref[here, :], weight)
            g, u = gu_ref[0, at, :units], gu_ref[0, at, units:]
            sig = jax.nn.sigmoid(g)
            dgu_ref[0, at, :units] = (dhid * u * sig * (1.0 + g * (1.0 - sig))).astype(BF)
            dgu_ref[0, at, units:] = (dhid * g * sig).astype(BF)

        tiles((own_in, peer_in), MLP_TILE, block)

    return call(
        kernel,
        "mlp_mid",
        (count,),
        [(x, None, None) for x in both] + [by_step(downs), by_step(gate_up)],
        [step_out((count, rows, 2 * units), BF)],
        flops=2 * count * rows * width * units,
        moved=26_000_000,
        exps=count * rows * units,
        deps=deps,
    )[0]


def back_out(values, weights, name, deps=()):
    count, rows, cols = values.shape
    width = weights.shape[3]
    tile = rows // 4

    def kernel(v_ref, w_ref, own_ref, peer_ref):
        t = pl.program_id(0)
        value = sum(dot(v_ref[r], w_ref[r].reshape(cols, width)) for r in range(count))

        @pl.when(t < 2)
        def _():
            own_ref[...] = value

        @pl.when(t >= 2)
        def _():
            peer_ref[...] = value.astype(BF)

    return call(
        kernel,
        name,
        (4,),
        [(values, (count, tile, cols), lambda t: (0, t, 0)), (weights, None, None)],
        [
            (shape((rows // 2, width), F32), (tile, width), lambda t: (jnp.minimum(t, 1), 0)),
            (shape((rows // 2, width), BF), (tile, width), lambda t: (jnp.maximum(t - 2, 0), 0)),
        ],
        flops=2 * count * rows * width * cols,
        moved=2 * values.size + 2 * weights.size + 3 * rows * width,
        deps=deps,
    )


ORDERS = {"x": ((1, 3), (0, 2)), "y": ((2, 3), (0, 1))}


def grad_split(place, pairs, parts, deps=()):
    half, width = pairs[0][0][0].shape
    rows, count = 2 * half, pairs[0][1].shape[0]
    last = [right.shape[2] == rows for _, right in pairs]
    widths = [right.shape[1 if flip else 2] for (_, right), flip in zip(pairs, last)]
    cols, strip, n = sum(widths), width // 8, len(pairs)

    def kernel(place, *refs):
        lefts, refs = refs[: 2 * n], refs[2 * n :]
        rights, refs = refs[:n], refs[n:]
        outs, refs = refs[: 2 * len(parts)], refs[2 * len(parts) :]
        turned, res = refs[:n], refs[n]

        @pl.when(pl.program_id(0) == 0)
        def _():
            for j, lt in enumerate(turned):
                lt[:, :half] = lefts[2 * j][...].T
                lt[:, half:] = lefts[2 * j + 1][...].T

        begin = 0
        for lt, right, size, flip in zip(turned, rights, widths, last):
            part = dot_nt(lt[...], right[0]) if flip else dot(lt[...], right[0])
            res[:, begin : begin + size] = part
            begin += size
        step = pl.program_id(0)
        for k, (begin, size, order, low, high) in enumerate(parts):

            @pl.when((step >= low) & (step < high))
            def _(k=k, begin=begin, size=size, order=order):
                for ref, blocks in zip(outs[2 * k : 2 * k + 2], ORDERS[order]):
                    for j, rel in enumerate(blocks):
                        for core in range(2):
                            first = ((place[0] ^ rel) * 2 + (place[1] ^ core)) * strip
                            rows_at = pl.ds(pl.multiple_of(first, 16), strip)
                            ref[j, 0, core] = res[rows_at, begin : begin + size].astype(BF)

    outs = []
    for _, size, _, low, high in parts:

        def index(z, low=low, high=high):
            return (0, jnp.clip(z, low, high - 1) - low, 0, 0, 0)

        out = (shape((2, high - low, 2, strip, size), BF), (2, 1, 2, strip, size), index)
        outs += [out, out]
    return call(
        kernel,
        "grad_split",
        (count,),
        [(x, None, None) for both, _ in pairs for x in both] + [by_step(right) for _, right in pairs],
        outs,
        scratch=[pltpu.VMEM((width, rows), BF)] * n + [pltpu.VMEM((width, cols), F32)],
        scalars=(place,),
        flops=2 * count * rows * width * cols,
        moved=2 * rows * width + 2 * count * rows * cols + 2 * count * width * cols,
        deps=deps,
    )


def assemble(place, base, chunks, deps=()):
    blocks, part, width = base.shape
    count = chunks[0][0].shape[0]

    def kernel(place, base, *refs):
        out = refs[-1]
        q = place[0]
        own = pl.program_id(0) == place[2]

        @pl.when(own)
        def _():
            out[0] = base[...]

        @pl.when(jnp.logical_not(own))
        def _():
            begin = 0
            for j in range(len(chunks)):
                near, fx, sy, fy, sx = refs[5 * j : 5 * j + 5]
                half, size = fx.shape[-2], near.shape[1]
                a, b = slice(begin, begin + half), slice(begin + half, begin + size)
                out[0, q, begin : begin + size] = near[0]
                out[0, q ^ 1, a] = fx[0, 0]
                out[0, q ^ 1, b] = sx[0, 0]
                out[0, q ^ 2, a] = fy[0, 0]
                out[0, q ^ 2, b] = sy[0, 0]
                out[0, q ^ 3, a] = fy[1, 0]
                out[0, q ^ 3, b] = sx[1, 0]
                begin += size

    def far(array, whole):
        def index(z, place):
            back = (place[2] + count - z) % count
            return (0 if whole else 1, jnp.maximum(back - 1, 0), 0, 0)

        return (array, (2 if whole else 1, 1) + array.shape[2:], index)

    ins = [(base, None, None)]
    for near, *others in chunks:
        ins += [(near, (1,) + near.shape[1:], lambda z, place: (z, 0, 0))] + [far(x, j > 1) for j, x in enumerate(others)]
    return call(
        kernel,
        "assemble",
        (count,),
        ins,
        [(shape((count,) + base.shape, BF), (1,) + base.shape, lambda z, place: (z, 0, 0, 0))],
        scalars=(place,),
        moved=4 * count * base.size,
        deps=deps,
        dynamic=True,
    )[0]


def place_heads(place, own, got, hw):
    strip = own.shape[0]

    def kernel(place, own, got, qkv_ref, out_ref):
        first = place[1] == 0
        low = jnp.where(first, own[...], got[...].astype(F32))
        high = jnp.where(first, got[...].astype(F32), own[...])
        for j in range(3):
            at = slice(j * hw, (j + 1) * hw)
            qkv_ref[j] = jnp.concatenate([low[:, at], high[:, at]], axis=1)
        out_ref[...] = jnp.concatenate([low[:, 3 * hw :], high[:, 3 * hw :]], axis=1)

    return call(
        kernel,
        "place_heads",
        (1,),
        [(own, None, None), (got, None, None)],
        [(shape((3, strip, 2 * hw), F32), None, None), (shape((strip, 2 * hw), F32), None, None)],
        scalars=(place,),
    )


def last_sums(arrived, early, bins, own_bins, cols, bias_cols):
    sources, images, width = early.shape[0], early.shape[1], early.shape[2]
    ends = [int(x) for x in np.cumsum([images * width] + [cols] * images + [bias_cols, 4])]
    table_rows = own_bins.shape[0]

    def kernel(got, early, bins, own_bins, ada_ref, b_ref, bias_ref, rms_ref, table_ref):
        ada, table, flat = 0.0, 0.0, 0.0
        for i in range(images):
            d_mod = got[:, ends[i] : ends[i + 1]]
            flat = flat + total(d_mod)
            ada = ada + dot_tn(d_mod.astype(BF), early[:, i, :].astype(BF))
            picks = jnp.where(own_bins[...] == bins[i : i + 1, :], 1.0, 0.0).astype(F32)
            d_cond = got[:, i * width : (i + 1) * width]
            table = table + jnp.dot(picks, d_cond, precision=EXACT, preferred_element_type=F32)
        ada_ref[...] = ada
        b_ref[...] = flat
        bias_ref[...] = total(got[:, ends[images] : ends[images + 1]])
        sums = total(got[:, ends[images + 1] :])
        rms_ref[...] = jnp.sqrt(sums[:, :3] / (sums[:, 3:] * width))
        table_ref[...] = table

    return call(
        kernel,
        "last_sums",
        (1,),
        [(x, None, None) for x in (arrived, early, bins, own_bins)],
        [
            (shape((cols, width), F32), None, None),
            (shape((1, cols), F32), None, None),
            (shape((1, bias_cols), F32), None, None),
            (shape((1, 3), F32), None, None),
            (shape((table_rows, width), F32), None, None),
        ],
    )


def ada_back(d_mod, w_ada, deps=()):
    images, wide = d_mod.shape
    width = w_ada.shape[0]
    padded = jnp.zeros((16, wide), BF).at[:images].set(d_mod.astype(BF))

    def kernel(d_ref, w_ref, out_ref):
        part = dot_nt(d_ref[...], w_ref[...])
        add_into(pl.program_id(0), out_ref, slice(None), part)

    return call(
        kernel,
        "ada_back",
        (wide // width,),
        [(padded, (16, width), lambda k: (0, k)), (w_ada, (width, width), lambda k: (0, k))],
        [(shape((16, width), F32), None, None)],
        flops=20_000_000_000,
        moved=2 * w_ada.size,
        deps=deps,
    )[0][:images]


def norm(x):
    centered = x - jnp.mean(x, axis=-1, keepdims=True)
    inverse = lax.rsqrt(jnp.mean(centered * centered, axis=-1, keepdims=True) + EPSILON)
    return centered * inverse, inverse


def norm_back(d_normed, normed, inverse, scale):
    d_hat = d_normed * (1.0 + scale)
    return inverse * (
        d_hat
        - jnp.mean(d_hat, axis=-1, keepdims=True)
        - normed * jnp.mean(d_hat * normed, axis=-1, keepdims=True)
    )


def total(x):
    return jnp.sum(x, axis=0, keepdims=True)


SHIFT_ONE, SCALE_ONE, GATE_ONE, SHIFT_TWO, SCALE_TWO, GATE_TWO = range(6)


def by_image(body, name, lengths, mod, rows_in, bias, outs, sums, deps=(), moved=1):
    images, _, width = mod.shape
    seq = rows_in[0].shape[0] // images
    count = len(rows_in)

    def kernel(lens, mod_ref, bias_ref, *refs):
        row_id = lax.broadcasted_iota(jnp.int32, (seq, 1), 0)
        mask = jnp.where(row_id < lens[pl.program_id(0)], 1.0, 0.0).astype(F32)
        values = [ref[...].astype(F32) for ref in refs[:count]]
        got = body(mask, [mod_ref[0, j : j + 1, :] for j in range(6)], bias_ref[...], *values)
        for ref, value in zip(refs[count:-1], got):
            ref[...] = value.astype(ref.dtype)
        for j, value in enumerate(got[len(outs) :]):
            refs[-1][0, j : j + 1, :] = value

    block = ((seq, width), lambda i: (i, 0))
    return call(
        kernel,
        name,
        (images,),
        [(mod, (1, 6, width), lambda i: (i, 0, 0)), (bias, None, None)]
        + [(x,) + block for x in rows_in],
        [(shape(rows_in[0].shape, dtype),) + block for dtype in outs]
        + [(shape((images, sums, width), F32), (1, sums, width), lambda i: (i, 0, 0))],
        scalars=(lengths,),
        flops=1,
        moved=moved,
        deps=deps,
    )


def pre_attention(mask, mod, bias, x, upstream):
    normed, _ = norm(x)
    dm = mask * mod[GATE_TWO] * upstream
    return normed * (1.0 + mod[SCALE_ONE]) + mod[SHIFT_ONE], dm, total(dm), total(mask * x * x)


def pre_mlp(mask, mod, bias, x, att_own, att_peer):
    gated = mask * mod[GATE_ONE] * (att_own + att_peer + bias)
    residual = x + gated
    normed, _ = norm(residual)
    return residual, normed * (1.0 + mod[SCALE_TWO]) + mod[SHIFT_TWO], total(gated * gated)


def post_mlp(mask, mod, bias, residual, upstream, mlp_own, mlp_peer):
    branch = mlp_own + mlp_peer + bias
    gated = mask * mod[GATE_TWO] * branch
    return residual + gated, total(mask * branch * upstream), total(gated * gated)


def back_mlp(mask, mod, bias, residual, upstream, att_own, att_peer, da_own, da_peer):
    normed, inverse = norm(residual)
    da = da_own + da_peer
    dh = upstream + norm_back(da, normed, inverse, mod[SCALE_TWO])
    d_att = mask * mod[GATE_ONE] * dh
    branch = att_own + att_peer + bias
    return dh, d_att, total(mask * branch * dh), total(da), total(da * normed), total(d_att)


def back_attention(mask, mod, bias, x, dh, da_own, da_peer):
    normed, inverse = norm(x)
    da = da_own + da_peer
    return dh + norm_back(da, normed, inverse, mod[SCALE_ONE]), total(da), total(da * normed)


def ring(count, shift):
    return [(i, (i + shift) % count) for i in range(count)]


def take(array, index, axis):
    return lax.dynamic_index_in_dim(array, index, axis, keepdims=False)


def local(
    sizes,
    patches,
    conditioning,
    time_bins,
    lengths,
    positions,
    time_table,
    w_ada,
    b_ada,
    w_qkv,
    w_out,
    branch_bias,
    w_gu,
    w_down,
    d_out,
):
    axes = tuple(sizes)
    ny, nx, nc, tn = sizes.values()
    square = nx == 2 and ny == 2
    at_y, at_x, at_c, at_z = (lax.axis_index(name) for name in axes)
    at_q = at_y * nx + at_x
    devices = ny * nx * nc * tn
    image_count, width = conditioning.shape
    rows = patches.shape[0]
    seq = rows // image_count
    heads = w_qkv.shape[2] // HD // nc
    hw = heads * HD
    units = w_gu.shape[2] // nc
    strip = width // (ny * nx * nc)
    place = jnp.stack([at_q, at_c, at_z]).astype(jnp.int32)
    swap = ring(2, 1)

    def peer(value):
        return lax.ppermute(value, "c", ring(nc, 1))

    def core_share(weight, axis):
        size = weight.shape[axis] // nc
        return lax.dynamic_slice_in_dim(weight, at_c * size, size, axis)

    def later(values, marks):
        return lax.optimization_barrier((values, marks))[0] if marks else values

    def along_z(piece):
        return lax.all_to_all(jnp.broadcast_to(piece[None], (tn,) + piece.shape), "z", 0, 0)

    def plane_parts(near):
        half = (near.shape[1] // 2 + 15) // 16 * 16
        others = [take(near, (at_z + tn - r) % tn, 0) for r in range(1, tn)]
        return jnp.stack([x[:half] for x in others]), jnp.stack([x[half:] for x in others])

    def plane_first(parts, *marks):
        first, second = parts
        first_x = lax.ppermute(first, "x", swap)
        second_y = lax.ppermute(second, "y", swap)
        first_x, second_y = later((first_x, second_y), marks)
        return jnp.stack([first, first_x]), jnp.stack([second, second_y])

    def plane_second(pairs, *marks):
        crossed = lax.ppermute(pairs[0], "y", swap), lax.ppermute(pairs[1], "x", swap)
        return later(crossed, marks)

    def chunk(near, pairs, crossed):
        return near, pairs[0], pairs[1], crossed[0], crossed[1]

    def plane_plain(near, base):
        whole = lax.all_gather(near, ("y", "x"), axis=1)
        return whole.reshape((tn,) + base.shape)

    qkv_t = w_qkv.transpose(1, 2, 0)
    if square:
        heads_piece = jnp.where(
            at_q < 3,
            lax.dynamic_slice(qkv_t, (jnp.minimum(at_q, 2), at_c * hw, 0), (1, hw, width))[0],
            core_share(w_out, 0),
        )
    heads_own = jnp.concatenate([core_share(qkv_t, 1), core_share(w_out, 0)[None]], axis=0)
    gu_own = core_share(w_gu.transpose(1, 2, 0), 1).reshape(4, units // 2, width)
    down_own = core_share(w_down, 0).reshape(4, units // 4, width)
    if square:
        near_heads = along_z(heads_piece)
    else:
        flat = lambda own: take(own.reshape(ny * nx, -1, width), at_q, 0)
        heads_all, gu_all, down_all = (
            plane_plain(along_z(flat(own)), own) for own in (heads_own, gu_own, down_own)
        )

    def reduce_first(pairs, parts, deps=()):
        outs = grad_split(place, pairs, parts, deps)
        sent, kept = tuple(outs[::2]), tuple(outs[1::2])
        got = tuple(lax.ppermute(x, part[2], swap) for x, part in zip(sent, parts))
        return (kept, got), sent

    def reduce_send(state, *marks):
        kept, got = later(state, marks)
        return tuple((k[1].astype(F32) + g[1].astype(F32)).astype(BF) for k, g in zip(kept, got))

    def reduce_second(state, sends, parts, *marks):
        other = {"x": "y", "y": "x"}
        got = tuple(lax.ppermute(x, other[part[2]], swap) for x, part in zip(sends, parts))
        got = later(got, marks)
        return tuple(
            (k[0].astype(F32) + g[0].astype(F32) + h.astype(F32)).astype(BF)
            for k, g, h in zip(*state, got)
        )

    def reduce_plain(pairs):
        flip = lambda right: right.swapaxes(1, 2) if right.shape[2] == 2 * rows else right
        full = jnp.concatenate(
            [
                jnp.einsum(
                    "rd,zrn->zdn", jnp.concatenate(both), flip(right), preferred_element_type=F32
                )
                for both, right in pairs
            ],
            axis=2,
        )
        full = full.astype(BF).reshape(full.shape[0], ny * nx, nc, strip, -1)
        summed = lax.psum_scatter(full, ("y", "x"), scatter_dimension=1, tiled=False)
        return jnp.stack([take(summed, at_c, 1), take(summed, 1 - at_c, 1)], axis=1)

    def reduce_z(rows, *marks):
        return later(lax.all_to_all(rows, "z", 0, 0), marks)

    def z_sends(rows):
        return [take(rows, (at_z + tn - r) % tn, 0) for r in range(tn)]

    def reduce_z_steps(sends, *marks):
        got = [lax.ppermute(sends[r], "z", ring(tn, -r)) for r in range(1, tn)]
        return jnp.stack([sends[0]] + list(later(got, marks)))

    def swap_core(arrived):
        summed = jnp.sum(arrived.astype(F32), axis=0)
        return summed[0], peer(summed[1].astype(BF))

    def reduce_core(arrived):
        summed = jnp.sum(arrived.astype(F32), axis=0)
        own, got = summed[0], peer(summed[1].astype(BF)).astype(F32)
        first = at_c == 0
        return jnp.stack([jnp.where(first, own, got), jnp.where(first, got, own)])

    bins = jnp.arange(time_table.shape[0], dtype=jnp.int32)
    onehot = (time_bins[:, None] == bins[None, :]).astype(F32)
    cond_vec = conditioning + jnp.dot(onehot, time_table, precision=EXACT)
    cond_sig = jax.nn.sigmoid(cond_vec)
    silu_low = (cond_vec * cond_sig).astype(BF)
    mod = (dot(silu_low, w_ada) + b_ada).reshape(image_count, 6, width)
    bias_attn, bias_mlp = branch_bias[None, :width], branch_bias[None, width:]
    elementwise = functools.partial(by_image, lengths=lengths, mod=mod)
    a1_own, dm_own, sums_pre = elementwise(
        pre_attention, "pre_attention", rows_in=(patches, d_out), bias=bias_attn, outs=(BF, BF), sums=2
    )
    a1_all = (a1_own, peer(a1_own))
    facts = jnp.concatenate([positions.reshape(-1), lengths])
    facts_peer = peer(facts)
    lens = jnp.concatenate([lengths, facts_peer[2 * rows :]])
    pos = jnp.concatenate([positions, facts_peer[: 2 * rows].reshape(2, rows)], axis=1).astype(F32)
    quarter = HD // 4
    frequency = 10000.0 ** (-jnp.arange(quarter, dtype=F32) / quarter)
    angle = pos[:, None, :] * frequency[None, :, None]
    cosine, sine = jnp.cos(angle), jnp.sin(angle)
    cos = jnp.concatenate([cosine[0], cosine[0], cosine[1], cosine[1]], axis=0)
    sin = jnp.concatenate([sine[0], sine[0], sine[1], sine[1]], axis=0)
    def spread(value):
        return lax.all_to_all(jnp.broadcast_to(value[None], (devices,) + value.shape), axes, 0, 0)

    early = jnp.concatenate([silu_low.astype(F32), time_bins[:, None].astype(F32)], axis=1)
    own_heads = attn_fwd(
        lens, place, a1_all, heads_own[None], 1, tn, (), (), cos, sin, heads, seq
    )

    def attend(deps):
        return attn_fwd(
            lens, place, a1_all, heads_all, tn - 1, tn, tuple(own_heads[:4]), own_heads[4:],
            cos, sin, heads, seq, deps=deps,
        )

    def into_mlp(deps):
        return elementwise(
            pre_mlp,
            "pre_mlp",
            rows_in=(patches,) + att,
            bias=bias_attn,
            outs=(F32, BF),
            sums=1,
            deps=deps,
        )

    if square:
        gu_piece, near_heads = later((take(gu_own, at_q, 0), near_heads), (a1_own,))
        near_gu = along_z(gu_piece)
        pairs_heads = plane_first(plane_parts(near_heads))
        crossed_heads = plane_second(pairs_heads, own_heads[4])
        near_gu = later(near_gu, (crossed_heads,))
        parts_gu = plane_parts(near_gu)
        down_piece = later(take(down_own, at_q, 0), (near_gu,))
        near_down = along_z(down_piece)
        heads_all = assemble(
            place, heads_own, [chunk(near_heads, pairs_heads, crossed_heads)], deps=parts_gu
        )
        pairs_gu = plane_first(parts_gu, heads_all)
        q, k, v, attended, att_own, att_peer = attend(pairs_gu)
        crossed_gu = plane_second(pairs_gu, att_own)
        near_down = later(near_down, (att_own,))
        parts_down = plane_parts(near_down)
        att = (att_own, peer(att_peer))
        residual, a2_own, sums_att = into_mlp(crossed_gu + parts_down)
        pairs_down = plane_first(parts_down, a2_own)
        gu_all = assemble(place, gu_own, [chunk(near_gu, pairs_gu, crossed_gu)], deps=(a2_own,))
        wait_mlp = pairs_down
    else:
        q, k, v, attended, att_own, att_peer = attend(())
        att = (att_own, peer(att_peer))
        residual, a2_own, sums_att = into_mlp(())
        wait_mlp = ()
    a2_all = (a2_own, peer(a2_own))
    dm_all = (dm_own, peer(dm_own))
    gate_up, hidden = mlp_fwd(a2_all, gu_all, deps=wait_mlp)

    def finish_mlp(deps):
        return elementwise(
            post_mlp,
            "post_mlp",
            rows_in=(residual, d_out, mlp_own, peer(mlp_peer)),
            bias=bias_mlp,
            outs=(F32,),
            sums=2,
            deps=deps,
        )

    def through_mlp(deps):
        return elementwise(
            back_mlp,
            "back_mlp",
            rows_in=(residual, d_out) + att + (da2_own, peer(da2_peer)),
            bias=bias_attn,
            outs=(F32, BF),
            sums=4,
            deps=deps,
            moved=30_000_000,
        )

    def back_heads(deps):
        return attn_bwd(
            lens, da_all, heads_all, (0, tn), (), cos, sin, q, k, v, heads, seq, deps=deps
        )

    def through_attention(deps):
        return elementwise(
            back_attention,
            "back_attention",
            rows_in=(patches, dh, da1_own, peer(da1_peer)),
            bias=bias_attn,
            outs=(F32,),
            sums=2,
            deps=deps,
        )

    if square:
        crossed_down = plane_second(pairs_down, hidden)
        mid = tn // 2
        down_parts = ((0, units, "x", 0, mid), (0, units, "y", mid, tn))
        gu_parts = (
            (0, units, "x", 0, mid),
            (units, units, "y", 0, mid),
            (0, units, "x", mid, tn),
            (units, units, "y", mid, tn),
        )
        rest = 4 * hw - 512
        heads_parts = (
            (0, 256, "x", 0, tn),
            (256, 256, "y", 0, tn),
            (512, rest, "x", 0, mid),
            (512, rest, "y", mid, tn),
        )
        down_state, down_sent = reduce_first([(dm_all, hidden)], down_parts, crossed_down)
        down_all = assemble(
            place, down_own, [chunk(near_down, pairs_down, crossed_down)], deps=down_sent
        )
        d_gate_up = mlp_mid(dm_all, down_all, gate_up, deps=down_sent)
        gu_state, gu_sent = reduce_first([(a2_all, d_gate_up)], gu_parts)
        one, two = ((gu_state[0][k : k + 2], gu_state[1][k : k + 2]) for k in (0, 2))
        down_sends = reduce_send(down_state, gu_sent)
        da2_own, da2_peer = back_out(d_gate_up, gu_all, "mlp_back", deps=gu_sent + down_sends)
        one_sends = reduce_send(one, da2_own)
        early_all = spread(later(early, (da2_own,)))
        dh, da_own, sums_back = through_mlp(one_sends)
        da_all = (da_own, peer(da_own))
        bins_all = early_all[:, :, width].T.astype(jnp.int32)
        two_sends = reduce_send(two, da_own)
        d_qkv, da1_own, da1_peer = back_heads((early_all,) + two_sends)
        heads_state, heads_sent = reduce_first(
            [(a1_all, d_qkv), (da_all, attended)], heads_parts, two_sends
        )
        one_rows = reduce_second(one, one_sends, gu_parts[:2], d_qkv, heads_sent)
        down_rows = reduce_second(down_state, down_sends, down_parts, heads_sent)
        two_rows = reduce_second(two, two_sends, gu_parts[2:], heads_sent)
        gu_rows = jnp.concatenate(
            [jnp.concatenate(half, axis=3) for half in (one_rows, two_rows)], axis=0
        )
        mlp_rows = jnp.concatenate([gu_rows, jnp.concatenate(down_rows, axis=0)], axis=3)
        d_inputs, sums_one = through_attention(heads_sent + (mlp_rows,))
        mlp_own, mlp_peer = back_out(hidden, down_all, "mlp_out", deps=(sums_one,))
        mlp_z = reduce_z(mlp_rows, mlp_own)
        heads_sends = reduce_send(heads_state, mlp_own)
        output, sums_mlp = finish_mlp(heads_sends)
        heads_rows = reduce_second(heads_state, heads_sends, heads_parts, sums_mlp)
        heads_rows = jnp.concatenate(
            heads_rows[:2] + (jnp.concatenate(heads_rows[2:], axis=0),), axis=3
        )
    else:
        early_all = spread(early)
        bins_all = early_all[:, :, width].T.astype(jnp.int32)
        d_gate_up = mlp_mid(dm_all, down_all, gate_up)
        da2_own, da2_peer = back_out(d_gate_up, gu_all, "mlp_back")
        dh, da_own, sums_back = through_mlp(())
        da_all = (da_own, peer(da_own))
        mlp_own, mlp_peer = back_out(hidden, down_all, "mlp_out")
        output, sums_mlp = finish_mlp(())
        d_qkv, da1_own, da1_peer = back_heads(())
        d_inputs, sums_one = through_attention(())
        grad_down, grad_gu = (
            reduce_core(reduce_z(reduce_plain(pairs)))
            for pairs in ([(dm_all, hidden)], [(a2_all, d_gate_up)])
        )
        swapped = swap_core(reduce_z(reduce_plain([(a1_all, d_qkv), (da_all, attended)])))

    d_mod = jnp.concatenate([sums_one, sums_back[:, :3], sums_mlp[:, :1]], axis=1)
    d_mod = d_mod.reshape(image_count, 6 * width)
    d_bias = jnp.concatenate([jnp.sum(sums_back[:, 3], axis=0), jnp.sum(sums_pre[:, 0], axis=0)])
    sums = jnp.stack(
        [
            jnp.sum(sums_pre[:, 1]),
            jnp.sum(sums_att),
            jnp.sum(sums_mlp[:, 1]),
            jnp.sum(lengths).astype(F32),
        ]
    )
    ada_cols, bias_cols = 6 * width // devices, 2 * width // devices
    ready = jnp.concatenate(
        [
            d_mod.reshape(image_count, devices, ada_cols).transpose(1, 0, 2).reshape(devices, -1),
            d_bias.reshape(devices, bias_cols),
            jnp.broadcast_to(sums[None], (devices, 4)),
        ],
        axis=1,
    )
    if square:
        heads_blocks = z_sends(heads_rows)
        d_silu = ada_back(d_mod, w_ada, deps=(ready, mlp_z) + tuple(heads_blocks))
    else:
        d_silu = ada_back(d_mod, w_ada)
    d_cond = d_silu * cond_sig * (1.0 + cond_vec * (1.0 - cond_sig))
    message = jnp.concatenate(
        [jnp.broadcast_to(d_cond.reshape(1, -1), (devices, image_count * width)), ready], axis=1
    )
    if square:
        heads_z = reduce_z_steps(heads_blocks, d_cond)
        message, heads_z, mlp_z = lax.optimization_barrier((message, heads_z, mlp_z))
        swapped = swap_core(heads_z)
        grad_mlp = reduce_core(mlp_z)
        grad_gu, grad_down = grad_mlp[:, :, : 2 * units], grad_mlp[:, :, 2 * units :]
    arrived = lax.all_to_all(message, axes, 0, 0, tiled=True)
    table_rows = time_table.shape[0] // devices
    flat = (at_q * nc + at_c) * tn + at_z
    own_bins = flat * table_rows + jnp.arange(table_rows, dtype=jnp.int32)
    grad_ada, grad_b_ada, grad_bias, rms_values, grad_table = last_sums(
        arrived, early_all[:, :, :width], bins_all, own_bins[:, None], ada_cols, bias_cols
    )

    def joined(value, parts):
        both = [value[j].reshape(strip, parts, -1) for j in range(nc)]
        return jnp.concatenate(both, axis=2)

    grad_qkv, grad_out = place_heads(place, *swapped, hw)

    return (
        output,
        d_inputs,
        d_cond,
        grad_qkv.transpose(1, 0, 2),
        grad_out.T,
        joined(grad_gu, 2),
        joined(grad_down, 1)[:, 0].T,
        grad_ada.T,
        grad_b_ada[0],
        grad_bias[0],
        grad_table,
        rms_values[0],
    )


def solution(mesh):
    groups, tn = mesh.shape["dp"], mesh.shape["tensor"]
    nc, nx = 2, 2
    sizes = {"y": groups // (nx * nc), "x": nx, "c": nc, "z": tn}
    fine = Mesh(mesh.devices.reshape(tuple(sizes.values())), tuple(sizes))
    dp = ("y", "x", "c")
    every = dp + ("z",)
    return jax.shard_map(
        functools.partial(local, sizes),
        mesh=fine,
        in_specs=(
            P(every, None),
            P(every, None),
            P(every),
            P(every),
            P(None, every),
            P(),
            P(),
            P(),
            P(None, None, "z"),
            P("z", None),
            P(),
            P(None, None, "z"),
            P("z", None),
            P(every, None),
        ),
        out_specs=(
            P(every, None),
            P(every, None),
            P(every, None),
            P(dp, None, "z"),
            P("z", dp),
            P(dp, None, "z"),
            P("z", dp),
            P(None, every),
            P(every),
            P(every),
            P(every, None),
            P(),
        ),
        check_vma=False,
    )
```

```python
import functools

import jax
import jax.numpy as jnp
import numpy as np
from jax import lax
from jax.experimental import pallas as pl
from jax.experimental.pallas import tpu as pltpu
from jax.sharding import Mesh
from jax.sharding import PartitionSpec as P

HD = 72
EXACT = lax.Precision.HIGHEST
EPSILON = 1e-06
NEG = -1e30
VMEM_LIMIT = 58 * 1024 * 1024
UNROLL = 4
MLP_TILE = 256
BF = jnp.bfloat16
F32 = jnp.float32
NT = (((1,), (1,)), ((), ()))
TN = (((0,), (0,)), ((), ()))


def dot(a, b):
    return jnp.dot(a, b, preferred_element_type=F32)


def dot_nt(a, b):
    return lax.dot_general(a, b, NT, preferred_element_type=F32)


def dot_tn(a, b):
    return lax.dot_general(a, b, TN, preferred_element_type=F32)


def call(kernel, name, grid, ins, outs, scratch=(), scalars=(), flops=0, moved=0, exps=0, deps=(), carry=(), dynamic=False):
    def spec(shape, block, index):
        if block is None:
            return pl.BlockSpec(shape, lambda *_: (0,) * len(shape))
        return pl.BlockSpec(block, index if dynamic else lambda *at: index(*at[: len(grid)]))

    arrays = [item[0] for item in ins]
    in_specs = [spec(item[0].shape, item[1], item[2]) for item in ins]
    out_specs = [spec(item[0].shape, item[1], item[2]) for item in outs]
    count_s, count_i, count_d = len(scalars), len(ins), len(deps) + len(carry)

    def body(*refs):
        kept = refs[: count_s + count_i] + refs[count_s + count_i + count_d :]
        kernel(*kept)

    return pl.pallas_call(
        body,
        grid_spec=pltpu.PrefetchScalarGridSpec(
            num_scalar_prefetch=count_s,
            grid=grid,
            in_specs=in_specs + [pl.BlockSpec(memory_space=pl.ANY)] * count_d,
            out_specs=out_specs,
            scratch_shapes=list(scratch),
        ),
        out_shape=[item[0] for item in outs],
        compiler_params=pltpu.CompilerParams(
            dimension_semantics=("arbitrary",) * len(grid), vmem_limit_bytes=VMEM_LIMIT
        ),
        cost_estimate=pl.CostEstimate(flops=flops, bytes_accessed=moved, transcendentals=exps),
        input_output_aliases={count_s + count_i + len(deps) + j: j for j in range(len(carry))},
        name=name,
    )(*scalars, *arrays, *deps, *carry)


def shape(dims, dtype):
    return jax.ShapeDtypeStruct(tuple(dims), dtype)


def swap_matrix(width):
    quarter = HD // 4
    out = np.zeros((width, width), np.float32)
    for lane in range(width):
        if (lane % HD) % (2 * quarter) < quarter:
            out[lane + quarter, lane] = -1.0
        else:
            out[lane - quarter, lane] = 1.0
    return out


def head_mask(heads, which, dtype):
    lane = lax.broadcasted_iota(jnp.int32, (1, heads * HD), 1)
    inside = (lane >= which * HD) & (lane < (which + 1) * HD)
    return jnp.where(inside, 1.0, 0.0).astype(F32).astype(dtype)


def finish(parts, outs, starts, tile):
    half = outs[0].shape[0]
    for j, ref in enumerate(outs):
        for t in range(half // tile):
            at = slice(t * tile, (t + 1) * tile)
            value = parts(slice(j * half + t * tile, j * half + (t + 1) * tile))
            if starts:
                value = value + starts[j][at, :]
            ref[at, :] = value.astype(ref.dtype)


def add_into(step, acc, rows, part):
    @pl.when(step == 0)
    def _():
        acc[rows, :] = part

    @pl.when(step > 0)
    def _():
        acc[rows, :] = acc[rows, :] + part


def at_step(step, count, body):
    for r in range(count):

        @pl.when(step == r)
        def _(r=r):
            body(r)


def halves_out(rows, width, last):
    return [(shape((rows, width), F32), None, None), (shape((rows, width), BF if last else F32), None, None)]


def by_step(array, begin=0):
    return (array, (1,) + array.shape[1:], lambda z: (z + begin,) + (0,) * (array.ndim - 1))


def step_out(dims, dtype):
    return (shape(dims, dtype), (1,) + tuple(dims[1:]), lambda z: (z,) + (0,) * (len(dims) - 1))


def attn_fwd(lens, place, both, weights, count, total, carry, starts, cos, sin, heads, seq, deps=()):
    (half, width), hw = both[0].shape, heads * HD
    ahead = 1 if carry else 0
    last = bool(carry)
    rows = 2 * half
    images, given = rows // seq, len(starts)
    scale = HD ** (-0.5)

    def kernel(lens, place, own_in, peer_in, cos_ref, sin_ref, swap_ref, w_ref, *refs):
        starts, refs = refs[:given], refs[given:]
        q_ref, k_ref, v_ref, o_ref, own_ref, peer_ref, wcat, wout, full, o_all = refs
        step = pl.program_id(0)
        for j in range(3):
            wcat[j * hw : (j + 1) * hw, :] = w_ref[0, j]
        wcat[3 * hw :, :] = dot(swap_ref[...], wcat[: 2 * hw, :]).astype(BF)
        full[:, :half] = dot_nt(wcat[...], own_in[...])
        full[:, half:] = dot_nt(wcat[...], peer_in[...])

        def image(i, carry):
            at = pl.ds(pl.multiple_of(i * seq, seq), seq)
            cos, sin = cos_ref[:, at], sin_ref[:, at]
            ok = lax.broadcasted_iota(jnp.int32, (seq, 1), 0) < lens[i]
            outs = []
            for h in range(heads):
                part = lambda j: full[j * hw + h * HD : j * hw + (h + 1) * HD, at]
                q = (part(0) * cos + part(3) * sin).astype(BF)
                k = (part(1) * cos + part(4) * sin).astype(BF)
                v = part(2).astype(BF)
                q_ref[0, h, :, at] = q
                k_ref[0, h, :, at] = k
                v_ref[0, h, :, at] = v
                st = jnp.where(ok, dot_tn(k, q) * scale, NEG)
                ex = jnp.exp(st - jnp.max(st, axis=0, keepdims=True))
                probs = (ex * (1.0 / jnp.sum(ex, axis=0, keepdims=True))).astype(BF)
                outs.append(dot(v, probs))
            o_ref[0, :, at] = jnp.concatenate(outs, axis=0).astype(BF)
            return carry

        lax.fori_loop(0, images, image, 0, unroll=UNROLL)

        def keep(r):
            wout[r * hw : (r + 1) * hw, :] = w_ref[0, 3]
            o_all[r * hw : (r + 1) * hw, :] = o_ref[0]

        at_step(step, count, keep)

        @pl.when(step == count - 1)
        def _():
            finish(lambda at: dot_tn(o_all[:, at], wout[...]), (own_ref, peer_ref), starts, seq)

    def block_of(step, lens, place):
        return (place[2] + ahead + step) % total

    def out(*dims):
        index = lambda *at: (block_of(*at),) + (0,) * len(dims)
        return (shape((total,) + dims, BF), (1,) + dims, index)

    index = (lambda *at: (block_of(*at), 0, 0, 0)) if carry else (lambda *at: (0, 0, 0, 0))
    return call(
        kernel,
        "attn_fwd",
        (count,),
        [(x, None, None) for x in both + (cos, sin, jnp.asarray(swap_matrix(2 * hw).T, BF))]
        + [(weights, (1,) + weights.shape[1:], index)]
        + [(x, None, None) for x in starts],
        [out(heads, HD, rows)] * 3 + [out(hw, rows)] + halves_out(half, width, last),
        scratch=[
            pltpu.VMEM((5 * hw, width), BF),
            pltpu.VMEM((count * hw, width), BF),
            pltpu.VMEM((5 * hw, rows), F32),
            pltpu.VMEM((count * hw, rows), BF),
        ],
        scalars=(lens, place),
        flops=2 * count * rows * width * 6 * hw + 8 * count * rows * heads * seq * 256,
        moved=20_000_000,
        exps=count * rows * heads * seq,
        deps=deps,
        carry=carry,
        dynamic=True,
    )


def attn_bwd(lens, both, weights, part_of, starts, cos, sin, q, k, v, heads, seq, deps=()):
    begin, end = part_of
    count, (half, width), hw = end - begin, both[0].shape, heads * HD
    last = end == weights.shape[0]
    rows = 2 * half
    images, given = rows // seq, len(starts)
    scale = HD ** (-0.5)

    def kernel(lens, own_in, peer_in, cos_ref, sin_ref, swap_ref, q_ref, k_ref, v_ref, w_ref, *refs):
        starts, refs = refs[:given], refs[given:]
        dqkv_ref, own_ref, peer_ref, w_all, do_all, d_all = refs
        step = pl.program_id(0)
        do_all[:, :half] = dot_nt(w_ref[0, 3], own_in[...])
        do_all[:, half:] = dot_nt(w_ref[0, 3], peer_in[...])

        def image(i, carry):
            at = pl.ds(pl.multiple_of(i * seq, seq), seq)
            cos, sin = cos_ref[:, at], sin_ref[:, at]
            ok = lax.broadcasted_iota(jnp.int32, (seq, 1), 0) < lens[i]
            dqs, dks, dvs = [], [], []
            for h in range(heads):
                do = do_all[h * HD : (h + 1) * HD, at].astype(BF)
                q, k, v = q_ref[0, h, :, at], k_ref[0, h, :, at], v_ref[0, h, :, at]
                st = jnp.where(ok, dot_tn(k, q) * scale, NEG)
                dp = dot_tn(v, do)
                ex = jnp.exp(st - jnp.max(st, axis=0, keepdims=True))
                probs = ex * (1.0 / jnp.sum(ex, axis=0, keepdims=True))
                inner = jnp.sum(dp * probs, axis=0, keepdims=True)
                ds = (probs * (dp - inner)).astype(BF)
                dvs.append(dot_nt(do, probs.astype(BF)))
                dk = dot_nt(q, ds), dot_nt(dot(swap_ref[...], q).astype(BF), ds)
                dq = dot(k, ds), dot(dot(swap_ref[...], k).astype(BF), ds)
                dqs.append((dq[0] * cos - dq[1] * sin) * scale)
                dks.append((dk[0] * cos - dk[1] * sin) * scale)
            dqkv_ref[0, :, at] = jnp.concatenate(dqs + dks + dvs, axis=0).astype(BF)
            return carry

        lax.fori_loop(0, images, image, 0, unroll=UNROLL)

        def keep(r):
            for j in range(3):
                first = (r * 3 + j) * hw
                w_all[first : first + hw, :] = w_ref[0, j]
            d_all[r * 3 * hw : (r + 1) * 3 * hw, :] = dqkv_ref[0]

        at_step(step, count, keep)

        @pl.when(step == count - 1)
        def _():
            finish(lambda at: dot_tn(d_all[:, at], w_all[...]), (own_ref, peer_ref), starts, seq)

    return call(
        kernel,
        "attn_bwd",
        (count,),
        [(x, None, None) for x in both + (cos, sin, jnp.asarray(swap_matrix(HD).T, BF))]
        + [by_step(q), by_step(k), by_step(v), by_step(weights, begin)]
        + [(x, None, None) for x in starts],
        [step_out((count, 3 * hw, rows), BF)] + halves_out(half, width, last),
        scratch=[
            pltpu.VMEM((count * 3 * hw, width), BF),
            pltpu.VMEM((hw, rows), F32),
            pltpu.VMEM((count * 3 * hw, rows), BF),
        ],
        scalars=(lens,),
        flops=2 * count * rows * width * 4 * hw + 20 * count * rows * heads * seq * 256,
        moved=20_000_000,
        exps=count * rows * heads * seq,
        deps=deps,
    )


def tiles(refs, tile, body):
    half = refs[0].shape[0]
    for j, ref in enumerate(refs):
        for t in range(half // tile):
            body(ref, slice(t * tile, (t + 1) * tile), slice(j * half + t * tile, j * half + (t + 1) * tile))


def mlp_fwd(both, weights, deps=()):
    count, blocks, part, width = weights.shape
    rows, cols = 2 * both[0].shape[0], blocks * part
    units = cols // 2

    def kernel(own_in, peer_in, w_ref, gu_ref, hid_ref):
        weight = w_ref[0].reshape(cols, width)

        def block(ref, here, at):
            gu = dot_nt(ref[here, :], weight)
            gu_ref[0, at, :] = gu
            g, u = gu[:, :units], gu[:, units:]
            hid_ref[0, at, :] = (g * jax.nn.sigmoid(g) * u).astype(BF)

        tiles((own_in, peer_in), MLP_TILE, block)

    return call(
        kernel,
        "mlp_fwd",
        (count,),
        [(x, None, None) for x in both] + [by_step(weights)],
        [step_out((count, rows, cols), F32), step_out((count, rows, units), BF)],
        flops=2 * count * rows * width * cols,
        moved=26_000_000,
        exps=count * rows * units,
        deps=deps,
    )


def mlp_mid(both, downs, gate_up, deps=()):
    count, blocks, part, width = downs.shape
    rows, units = 2 * both[0].shape[0], blocks * part

    def kernel(own_in, peer_in, w_ref, gu_ref, dgu_ref):
        weight = w_ref[0].reshape(units, width)

        def block(ref, here, at):
            dhid = dot_nt(ref[here, :], weight)
            g, u = gu_ref[0, at, :units], gu_ref[0, at, units:]
            sig = jax.nn.sigmoid(g)
            dgu_ref[0, at, :units] = (dhid * u * sig * (1.0 + g * (1.0 - sig))).astype(BF)
            dgu_ref[0, at, units:] = (dhid * g * sig).astype(BF)

        tiles((own_in, peer_in), MLP_TILE, block)

    return call(
        kernel,
        "mlp_mid",
        (count,),
        [(x, None, None) for x in both] + [by_step(downs), by_step(gate_up)],
        [step_out((count, rows, 2 * units), BF)],
        flops=2 * count * rows * width * units,
        moved=26_000_000,
        exps=count * rows * units,
        deps=deps,
    )[0]


def back_out(values, weights, name, deps=()):
    count, rows, cols = values.shape
    width = weights.shape[3]
    tile = rows // 4

    def kernel(v_ref, w_ref, own_ref, peer_ref):
        t = pl.program_id(0)
        value = sum(dot(v_ref[r], w_ref[r].reshape(cols, width)) for r in range(count))

        @pl.when(t < 2)
        def _():
            own_ref[...] = value

        @pl.when(t >= 2)
        def _():
            peer_ref[...] = value.astype(BF)

    return call(
        kernel,
        name,
        (4,),
        [(values, (count, tile, cols), lambda t: (0, t, 0)), (weights, None, None)],
        [
            (shape((rows // 2, width), F32), (tile, width), lambda t: (jnp.minimum(t, 1), 0)),
            (shape((rows // 2, width), BF), (tile, width), lambda t: (jnp.maximum(t - 2, 0), 0)),
        ],
        flops=2 * count * rows * width * cols,
        moved=2 * values.size + 2 * weights.size + 3 * rows * width,
        deps=deps,
    )


ORDERS = {"x": ((1, 3), (0, 2)), "y": ((2, 3), (0, 1))}


def grad_split(place, pairs, parts, deps=()):
    half, width = pairs[0][0][0].shape
    rows, count = 2 * half, pairs[0][1].shape[0]
    last = [right.shape[2] == rows for _, right in pairs]
    widths = [right.shape[1 if flip else 2] for (_, right), flip in zip(pairs, last)]
    cols, strip, n = sum(widths), width // 8, len(pairs)

    def kernel(place, *refs):
        lefts, refs = refs[: 2 * n], refs[2 * n :]
        rights, refs = refs[:n], refs[n:]
        outs, refs = refs[: 2 * len(parts)], refs[2 * len(parts) :]
        turned, res = refs[:n], refs[n]

        @pl.when(pl.program_id(0) == 0)
        def _():
            for j, lt in enumerate(turned):
                lt[:, :half] = lefts[2 * j][...].T
                lt[:, half:] = lefts[2 * j + 1][...].T

        begin = 0
        for lt, right, size, flip in zip(turned, rights, widths, last):
            part = dot_nt(lt[...], right[0]) if flip else dot(lt[...], right[0])
            res[:, begin : begin + size] = part
            begin += size
        step = pl.program_id(0)
        for k, (begin, size, order, low, high) in enumerate(parts):

            @pl.when((step >= low) & (step < high))
            def _(k=k, begin=begin, size=size, order=order):
                for ref, blocks in zip(outs[2 * k : 2 * k + 2], ORDERS[order]):
                    for j, rel in enumerate(blocks):
                        for core in range(2):
                            first = ((place[0] ^ rel) * 2 + (place[1] ^ core)) * strip
                            rows_at = pl.ds(pl.multiple_of(first, 16), strip)
                            ref[j, 0, core] = res[rows_at, begin : begin + size].astype(BF)

    outs = []
    for _, size, _, low, high in parts:

        def index(z, low=low, high=high):
            return (0, jnp.clip(z, low, high - 1) - low, 0, 0, 0)

        out = (shape((2, high - low, 2, strip, size), BF), (2, 1, 2, strip, size), index)
        outs += [out, out]
    return call(
        kernel,
        "grad_split",
        (count,),
        [(x, None, None) for both, _ in pairs for x in both] + [by_step(right) for _, right in pairs],
        outs,
        scratch=[pltpu.VMEM((width, rows), BF)] * n + [pltpu.VMEM((width, cols), F32)],
        scalars=(place,),
        flops=2 * count * rows * width * cols,
        moved=2 * rows * width + 2 * count * rows * cols + 2 * count * width * cols,
        deps=deps,
    )


def assemble(place, base, chunks, deps=()):
    blocks, part, width = base.shape
    count = chunks[0][0].shape[0]

    def kernel(place, base, *refs):
        out = refs[-1]
        q = place[0]
        own = pl.program_id(0) == place[2]

        @pl.when(own)
        def _():
            out[0] = base[...]

        @pl.when(jnp.logical_not(own))
        def _():
            begin = 0
            for j in range(len(chunks)):
                near, fx, sy, fy, sx = refs[5 * j : 5 * j + 5]
                half, size = fx.shape[-2], near.shape[1]
                a, b = slice(begin, begin + half), slice(begin + half, begin + size)
                out[0, q, begin : begin + size] = near[0]
                out[0, q ^ 1, a] = fx[0, 0]
                out[0, q ^ 1, b] = sx[0, 0]
                out[0, q ^ 2, a] = fy[0, 0]
                out[0, q ^ 2, b] = sy[0, 0]
                out[0, q ^ 3, a] = fy[1, 0]
                out[0, q ^ 3, b] = sx[1, 0]
                begin += size

    def far(array, whole):
        def index(z, place):
            back = (place[2] + count - z) % count
            return (0 if whole else 1, jnp.maximum(back - 1, 0), 0, 0)

        return (array, (2 if whole else 1, 1) + array.shape[2:], index)

    ins = [(base, None, None)]
    for near, *others in chunks:
        ins += [(near, (1,) + near.shape[1:], lambda z, place: (z, 0, 0))] + [far(x, j > 1) for j, x in enumerate(others)]
    return call(
        kernel,
        "assemble",
        (count,),
        ins,
        [(shape((count,) + base.shape, BF), (1,) + base.shape, lambda z, place: (z, 0, 0, 0))],
        scalars=(place,),
        moved=4 * count * base.size,
        deps=deps,
        dynamic=True,
    )[0]


def place_heads(place, own, got, hw):
    strip = own.shape[0]

    def kernel(place, own, got, qkv_ref, out_ref):
        first = place[1] == 0
        low = jnp.where(first, own[...], got[...].astype(F32))
        high = jnp.where(first, got[...].astype(F32), own[...])
        for j in range(3):
            at = slice(j * hw, (j + 1) * hw)
            qkv_ref[j] = jnp.concatenate([low[:, at], high[:, at]], axis=1)
        out_ref[...] = jnp.concatenate([low[:, 3 * hw :], high[:, 3 * hw :]], axis=1)

    return call(
        kernel,
        "place_heads",
        (1,),
        [(own, None, None), (got, None, None)],
        [(shape((3, strip, 2 * hw), F32), None, None), (shape((strip, 2 * hw), F32), None, None)],
        scalars=(place,),
    )


def last_sums(arrived, own_bins, images, width, cols, bias_cols):
    sizes = [images * width, images * width] + [cols] * images + [bias_cols, 4]
    ends = [int(x) for x in np.cumsum(sizes)]
    table_rows = own_bins.shape[1]

    def kernel(got, own_bins, ada_ref, b_ref, bias_ref, rms_ref, table_ref):
        ada, table, flat = 0.0, 0.0, 0.0
        for i in range(images):
            d_mod = got[:, ends[1 + i] : ends[2 + i]]
            flat = flat + total(d_mod)
            silu = got[:, ends[0] + i * width : ends[0] + (i + 1) * width]
            ada = ada + dot_tn(d_mod.astype(BF), silu.astype(BF))
            bins = got[:, ends[-1] + i : ends[-1] + i + 1]
            picks = jnp.where(own_bins[...] == bins, 1.0, 0.0).astype(F32)
            table = table + lax.dot_general(
                picks,
                got[:, i * width : (i + 1) * width],
                TN,
                precision=EXACT,
                preferred_element_type=F32,
            )
        ada_ref[...] = ada
        b_ref[...] = flat
        bias_ref[...] = total(got[:, ends[-3] : ends[-2]])
        sums = total(got[:, ends[-2] : ends[-1]])
        rms_ref[...] = jnp.sqrt(sums[:, :3] / (sums[:, 3:] * width))
        table_ref[...] = table

    return call(
        kernel,
        "last_sums",
        (1,),
        [(x, None, None) for x in (arrived, own_bins)],
        [
            (shape((cols, width), F32), None, None),
            (shape((1, cols), F32), None, None),
            (shape((1, bias_cols), F32), None, None),
            (shape((1, 3), F32), None, None),
            (shape((table_rows, width), F32), None, None),
        ],
    )


def ada_back(d_mod, w_ada, deps=()):
    images, wide = d_mod.shape
    width = w_ada.shape[0]
    padded = jnp.zeros((16, wide), BF).at[:images].set(d_mod.astype(BF))

    def kernel(d_ref, w_ref, out_ref):
        part = dot_nt(d_ref[...], w_ref[...])
        add_into(pl.program_id(0), out_ref, slice(None), part)

    return call(
        kernel,
        "ada_back",
        (wide // width,),
        [(padded, (16, width), lambda k: (0, k)), (w_ada, (width, width), lambda k: (0, k))],
        [(shape((16, width), F32), None, None)],
        flops=20_000_000_000,
        moved=2 * w_ada.size,
        deps=deps,
    )[0][:images]


def norm(x):
    centered = x - jnp.mean(x, axis=-1, keepdims=True)
    inverse = lax.rsqrt(jnp.mean(centered * centered, axis=-1, keepdims=True) + EPSILON)
    return centered * inverse, inverse


def norm_back(d_normed, normed, inverse, scale):
    d_hat = d_normed * (1.0 + scale)
    return inverse * (
        d_hat
        - jnp.mean(d_hat, axis=-1, keepdims=True)
        - normed * jnp.mean(d_hat * normed, axis=-1, keepdims=True)
    )


def total(x):
    return jnp.sum(x, axis=0, keepdims=True)


SHIFT_ONE, SCALE_ONE, GATE_ONE, SHIFT_TWO, SCALE_TWO, GATE_TWO = range(6)


def by_image(body, name, lengths, mod, rows_in, bias, outs, sums, deps=(), moved=1):
    images, _, width = mod.shape
    seq = rows_in[0].shape[0] // images
    count = len(rows_in)

    def kernel(lens, mod_ref, bias_ref, *refs):
        row_id = lax.broadcasted_iota(jnp.int32, (seq, 1), 0)
        mask = jnp.where(row_id < lens[pl.program_id(0)], 1.0, 0.0).astype(F32)
        values = [ref[...].astype(F32) for ref in refs[:count]]
        got = body(mask, [mod_ref[0, j : j + 1, :] for j in range(6)], bias_ref[...], *values)
        for ref, value in zip(refs[count:-1], got):
            ref[...] = value.astype(ref.dtype)
        for j, value in enumerate(got[len(outs) :]):
            refs[-1][0, j : j + 1, :] = value

    block = ((seq, width), lambda i: (i, 0))
    return call(
        kernel,
        name,
        (images,),
        [(mod, (1, 6, width), lambda i: (i, 0, 0)), (bias, None, None)]
        + [(x,) + block for x in rows_in],
        [(shape(rows_in[0].shape, dtype),) + block for dtype in outs]
        + [(shape((images, sums, width), F32), (1, sums, width), lambda i: (i, 0, 0))],
        scalars=(lengths,),
        flops=1,
        moved=moved,
        deps=deps,
    )


def pre_attention(mask, mod, bias, x, upstream):
    normed, _ = norm(x)
    dm = mask * mod[GATE_TWO] * upstream
    return normed * (1.0 + mod[SCALE_ONE]) + mod[SHIFT_ONE], dm, total(dm), total(mask * x * x)


def pre_mlp(mask, mod, bias, x, att_own, att_peer):
    gated = mask * mod[GATE_ONE] * (att_own + att_peer + bias)
    residual = x + gated
    normed, _ = norm(residual)
    return residual, normed * (1.0 + mod[SCALE_TWO]) + mod[SHIFT_TWO], total(gated * gated)


def post_mlp(mask, mod, bias, residual, upstream, mlp_own, mlp_peer):
    branch = mlp_own + mlp_peer + bias
    gated = mask * mod[GATE_TWO] * branch
    return residual + gated, total(mask * branch * upstream), total(gated * gated)


def back_mlp(mask, mod, bias, residual, upstream, att_own, att_peer, da_own, da_peer):
    normed, inverse = norm(residual)
    da = da_own + da_peer
    dh = upstream + norm_back(da, normed, inverse, mod[SCALE_TWO])
    d_att = mask * mod[GATE_ONE] * dh
    branch = att_own + att_peer + bias
    return dh, d_att, total(mask * branch * dh), total(da), total(da * normed), total(d_att)


def back_attention(mask, mod, bias, x, dh, da_own, da_peer):
    normed, inverse = norm(x)
    da = da_own + da_peer
    return dh + norm_back(da, normed, inverse, mod[SCALE_ONE]), total(da), total(da * normed)


def ring(count, shift):
    return [(i, (i + shift) % count) for i in range(count)]


def take(array, index, axis):
    return lax.dynamic_index_in_dim(array, index, axis, keepdims=False)


def local(
    sizes,
    patches,
    conditioning,
    time_bins,
    lengths,
    positions,
    time_table,
    w_ada,
    b_ada,
    w_qkv,
    w_out,
    branch_bias,
    w_gu,
    w_down,
    d_out,
):
    axes = tuple(sizes)
    ny, nx, nc, tn = sizes.values()
    square = nx == 2 and ny == 2
    at_y, at_x, at_c, at_z = (lax.axis_index(name) for name in axes)
    at_q = at_y * nx + at_x
    devices = ny * nx * nc * tn
    image_count, width = conditioning.shape
    rows = patches.shape[0]
    seq = rows // image_count
    heads = w_qkv.shape[2] // HD // nc
    hw = heads * HD
    units = w_gu.shape[2] // nc
    strip = width // (ny * nx * nc)
    place = jnp.stack([at_q, at_c, at_z]).astype(jnp.int32)
    swap = ring(2, 1)

    def peer(value):
        return lax.ppermute(value, "c", ring(nc, 1))

    def core_share(weight, axis):
        size = weight.shape[axis] // nc
        return lax.dynamic_slice_in_dim(weight, at_c * size, size, axis)

    def later(values, marks):
        return lax.optimization_barrier((values, marks))[0] if marks else values

    def along_z(piece):
        return lax.all_to_all(jnp.broadcast_to(piece[None], (tn,) + piece.shape), "z", 0, 0)

    def plane_parts(near):
        half = (near.shape[1] // 2 + 15) // 16 * 16
        others = [take(near, (at_z + tn - r) % tn, 0) for r in range(1, tn)]
        return jnp.stack([x[:half] for x in others]), jnp.stack([x[half:] for x in others])

    def plane_first(parts, *marks):
        first, second = parts
        first_x = lax.ppermute(first, "x", swap)
        second_y = lax.ppermute(second, "y", swap)
        first_x, second_y = later((first_x, second_y), marks)
        return jnp.stack([first, first_x]), jnp.stack([second, second_y])

    def plane_second(pairs, *marks):
        crossed = lax.ppermute(pairs[0], "y", swap), lax.ppermute(pairs[1], "x", swap)
        return later(crossed, marks)

    def chunk(near, pairs, crossed):
        return near, pairs[0], pairs[1], crossed[0], crossed[1]

    def plane_plain(near, base):
        whole = lax.all_gather(near, ("y", "x"), axis=1)
        return whole.reshape((tn,) + base.shape)

    qkv_t = w_qkv.transpose(1, 2, 0)
    if square:
        heads_piece = jnp.where(
            at_q < 3,
            lax.dynamic_slice(qkv_t, (jnp.minimum(at_q, 2), at_c * hw, 0), (1, hw, width))[0],
            core_share(w_out, 0),
        )
    heads_own = jnp.concatenate([core_share(qkv_t, 1), core_share(w_out, 0)[None]], axis=0)
    gu_own = core_share(w_gu.transpose(1, 2, 0), 1).reshape(4, units // 2, width)
    down_own = core_share(w_down, 0).reshape(4, units // 4, width)
    if square:
        near_heads = along_z(heads_piece)
    else:
        flat = lambda own: take(own.reshape(ny * nx, -1, width), at_q, 0)
        heads_all, gu_all, down_all = (
            plane_plain(along_z(flat(own)), own) for own in (heads_own, gu_own, down_own)
        )

    def reduce_first(pairs, parts, deps=()):
        outs = grad_split(place, pairs, parts, deps)
        sent, kept = tuple(outs[::2]), tuple(outs[1::2])
        got = tuple(lax.ppermute(x, part[2], swap) for x, part in zip(sent, parts))
        return (kept, got), sent

    def reduce_send(state, *marks):
        kept, got = later(state, marks)
        return tuple((k[1].astype(F32) + g[1].astype(F32)).astype(BF) for k, g in zip(kept, got))

    def reduce_second(state, sends, parts, *marks):
        other = {"x": "y", "y": "x"}
        got = tuple(lax.ppermute(x, other[part[2]], swap) for x, part in zip(sends, parts))
        got = later(got, marks)
        return tuple(
            (k[0].astype(F32) + g[0].astype(F32) + h.astype(F32)).astype(BF)
            for k, g, h in zip(*state, got)
        )

    def reduce_plain(pairs):
        flip = lambda right: right.swapaxes(1, 2) if right.shape[2] == 2 * rows else right
        full = jnp.concatenate(
            [
                jnp.einsum(
                    "rd,zrn->zdn", jnp.concatenate(both), flip(right), preferred_element_type=F32
                )
                for both, right in pairs
            ],
            axis=2,
        )
        full = full.astype(BF).reshape(full.shape[0], ny * nx, nc, strip, -1)
        summed = lax.psum_scatter(full, ("y", "x"), scatter_dimension=1, tiled=False)
        return jnp.stack([take(summed, at_c, 1), take(summed, 1 - at_c, 1)], axis=1)

    def reduce_z(rows, *marks):
        return later(lax.all_to_all(rows, "z", 0, 0), marks)

    def z_sends(rows):
        return [take(rows, (at_z + tn - r) % tn, 0) for r in range(tn)]

    def reduce_z_steps(sends, *marks):
        got = [lax.ppermute(sends[r], "z", ring(tn, -r)) for r in range(1, tn)]
        return jnp.stack([sends[0]] + list(later(got, marks)))

    def swap_core(arrived):
        summed = jnp.sum(arrived.astype(F32), axis=0)
        return summed[0], peer(summed[1].astype(BF))

    def reduce_core(arrived):
        summed = jnp.sum(arrived.astype(F32), axis=0)
        own, got = summed[0], peer(summed[1].astype(BF)).astype(F32)
        first = at_c == 0
        return jnp.stack([jnp.where(first, own, got), jnp.where(first, got, own)])

    bins = jnp.arange(time_table.shape[0], dtype=jnp.int32)
    onehot = (time_bins[:, None] == bins[None, :]).astype(F32)
    cond_vec = conditioning + jnp.dot(onehot, time_table, precision=EXACT)
    cond_sig = jax.nn.sigmoid(cond_vec)
    silu_low = (cond_vec * cond_sig).astype(BF)
    mod = (dot(silu_low, w_ada) + b_ada).reshape(image_count, 6, width)
    bias_attn, bias_mlp = branch_bias[None, :width], branch_bias[None, width:]
    elementwise = functools.partial(by_image, lengths=lengths, mod=mod)
    a1_own, dm_own, sums_pre = elementwise(
        pre_attention, "pre_attention", rows_in=(patches, d_out), bias=bias_attn, outs=(BF, BF), sums=2
    )
    a1_all = (a1_own, peer(a1_own))
    facts = jnp.concatenate([positions.reshape(-1), lengths])
    facts_peer = peer(facts)
    lens = jnp.concatenate([lengths, facts_peer[2 * rows :]])
    pos = jnp.concatenate([positions, facts_peer[: 2 * rows].reshape(2, rows)], axis=1).astype(F32)
    quarter = HD // 4
    frequency = 10000.0 ** (-jnp.arange(quarter, dtype=F32) / quarter)
    angle = pos[:, None, :] * frequency[None, :, None]
    cosine, sine = jnp.cos(angle), jnp.sin(angle)
    cos = jnp.concatenate([cosine[0], cosine[0], cosine[1], cosine[1]], axis=0)
    sin = jnp.concatenate([sine[0], sine[0], sine[1], sine[1]], axis=0)
    own_heads = attn_fwd(
        lens, place, a1_all, heads_own[None], 1, tn, (), (), cos, sin, heads, seq
    )

    def attend(deps):
        return attn_fwd(
            lens, place, a1_all, heads_all, tn - 1, tn, tuple(own_heads[:4]), own_heads[4:],
            cos, sin, heads, seq, deps=deps,
        )

    def into_mlp(deps):
        return elementwise(
            pre_mlp,
            "pre_mlp",
            rows_in=(patches,) + att,
            bias=bias_attn,
            outs=(F32, BF),
            sums=1,
            deps=deps,
        )

    if square:
        gu_piece, near_heads = later((take(gu_own, at_q, 0), near_heads), (a1_own,))
        near_gu = along_z(gu_piece)
        pairs_heads = plane_first(plane_parts(near_heads))
        crossed_heads = plane_second(pairs_heads, own_heads[4])
        near_gu = later(near_gu, (crossed_heads,))
        parts_gu = plane_parts(near_gu)
        down_piece = later(take(down_own, at_q, 0), (near_gu,))
        near_down = along_z(down_piece)
        heads_all = assemble(
            place, heads_own, [chunk(near_heads, pairs_heads, crossed_heads)], deps=parts_gu
        )
        pairs_gu = plane_first(parts_gu, heads_all)
        q, k, v, attended, att_own, att_peer = attend(pairs_gu)
        crossed_gu = plane_second(pairs_gu, att_own)
        near_down = later(near_down, (att_own,))
        parts_down = plane_parts(near_down)
        att = (att_own, peer(att_peer))
        residual, a2_own, sums_att = into_mlp(crossed_gu + parts_down)
        pairs_down = plane_first(parts_down, a2_own)
        gu_all = assemble(place, gu_own, [chunk(near_gu, pairs_gu, crossed_gu)], deps=(a2_own,))
        wait_mlp = pairs_down
    else:
        q, k, v, attended, att_own, att_peer = attend(())
        att = (att_own, peer(att_peer))
        residual, a2_own, sums_att = into_mlp(())
        wait_mlp = ()
    a2_all = (a2_own, peer(a2_own))
    dm_all = (dm_own, peer(dm_own))
    gate_up, hidden = mlp_fwd(a2_all, gu_all, deps=wait_mlp)

    def finish_mlp(deps):
        return elementwise(
            post_mlp,
            "post_mlp",
            rows_in=(residual, d_out, mlp_own, peer(mlp_peer)),
            bias=bias_mlp,
            outs=(F32,),
            sums=2,
            deps=deps,
        )

    def through_mlp(deps):
        return elementwise(
            back_mlp,
            "back_mlp",
            rows_in=(residual, d_out) + att + (da2_own, peer(da2_peer)),
            bias=bias_attn,
            outs=(F32, BF),
            sums=4,
            deps=deps,
            moved=30_000_000,
        )

    def back_heads(deps):
        return attn_bwd(
            lens, da_all, heads_all, (0, tn), (), cos, sin, q, k, v, heads, seq, deps=deps
        )

    def through_attention(deps):
        return elementwise(
            back_attention,
            "back_attention",
            rows_in=(patches, dh, da1_own, peer(da1_peer)),
            bias=bias_attn,
            outs=(F32,),
            sums=2,
            deps=deps,
        )

    if square:
        crossed_down = plane_second(pairs_down, hidden)
        mid = tn // 2
        down_parts = ((0, units, "x", 0, mid), (0, units, "y", mid, tn))
        gu_parts = (
            (0, units, "x", 0, mid),
            (units, units, "y", 0, mid),
            (0, units, "x", mid, tn),
            (units, units, "y", mid, tn),
        )
        rest = 4 * hw - 512
        heads_parts = (
            (0, 256, "x", 0, tn),
            (256, 256, "y", 0, tn),
            (512, rest, "x", 0, mid),
            (512, rest, "y", mid, tn),
        )
        down_state, down_sent = reduce_first([(dm_all, hidden)], down_parts, crossed_down)
        down_all = assemble(
            place, down_own, [chunk(near_down, pairs_down, crossed_down)], deps=down_sent
        )
        d_gate_up = mlp_mid(dm_all, down_all, gate_up, deps=down_sent)
        gu_state, gu_sent = reduce_first([(a2_all, d_gate_up)], gu_parts)
        one, two = ((gu_state[0][k : k + 2], gu_state[1][k : k + 2]) for k in (0, 2))
        down_sends = reduce_send(down_state, gu_sent)
        da2_own, da2_peer = back_out(d_gate_up, gu_all, "mlp_back", deps=gu_sent + down_sends)
        one_sends = reduce_send(one, da2_own)
        dh, da_own, sums_back = through_mlp(one_sends)
        da_all = (da_own, peer(da_own))
        two_sends = reduce_send(two, da_own)
        d_qkv, da1_own, da1_peer = back_heads(two_sends)
        heads_state, heads_sent = reduce_first(
            [(a1_all, d_qkv), (da_all, attended)], heads_parts, two_sends
        )
        one_rows = reduce_second(one, one_sends, gu_parts[:2], d_qkv, heads_sent)
        down_rows = reduce_second(down_state, down_sends, down_parts, heads_sent)
        two_rows = reduce_second(two, two_sends, gu_parts[2:], heads_sent)
        gu_rows = jnp.concatenate(
            [jnp.concatenate(half, axis=3) for half in (one_rows, two_rows)], axis=0
        )
        mlp_rows = jnp.concatenate([gu_rows, jnp.concatenate(down_rows, axis=0)], axis=3)
        d_inputs, sums_one = through_attention(heads_sent + (mlp_rows,))
        mlp_own, mlp_peer = back_out(hidden, down_all, "mlp_out", deps=(sums_one,))
        mlp_z = reduce_z(mlp_rows, mlp_own)
        heads_sends = reduce_send(heads_state, mlp_own)
        output, sums_mlp = finish_mlp(heads_sends)
        heads_rows = reduce_second(heads_state, heads_sends, heads_parts, sums_mlp)
        heads_rows = jnp.concatenate(
            heads_rows[:2] + (jnp.concatenate(heads_rows[2:], axis=0),), axis=3
        )
    else:
        d_gate_up = mlp_mid(dm_all, down_all, gate_up)
        da2_own, da2_peer = back_out(d_gate_up, gu_all, "mlp_back")
        dh, da_own, sums_back = through_mlp(())
        da_all = (da_own, peer(da_own))
        mlp_own, mlp_peer = back_out(hidden, down_all, "mlp_out")
        output, sums_mlp = finish_mlp(())
        d_qkv, da1_own, da1_peer = back_heads(())
        d_inputs, sums_one = through_attention(())
        grad_down, grad_gu = (
            reduce_core(reduce_z(reduce_plain(pairs)))
            for pairs in ([(dm_all, hidden)], [(a2_all, d_gate_up)])
        )
        swapped = swap_core(reduce_z(reduce_plain([(a1_all, d_qkv), (da_all, attended)])))

    d_mod = jnp.concatenate([sums_one, sums_back[:, :3], sums_mlp[:, :1]], axis=1)
    d_mod = d_mod.reshape(image_count, 6 * width)
    d_bias = jnp.concatenate([jnp.sum(sums_back[:, 3], axis=0), jnp.sum(sums_pre[:, 0], axis=0)])
    sums = jnp.stack(
        [
            jnp.sum(sums_pre[:, 1]),
            jnp.sum(sums_att),
            jnp.sum(sums_mlp[:, 1]),
            jnp.sum(lengths).astype(F32),
        ]
    )
    ada_cols, bias_cols = 6 * width // devices, 2 * width // devices
    ready = jnp.concatenate(
        [
            d_mod.reshape(image_count, devices, ada_cols).transpose(1, 0, 2).reshape(devices, -1),
            d_bias.reshape(devices, bias_cols),
            jnp.broadcast_to(sums[None], (devices, 4)),
            jnp.broadcast_to(time_bins.astype(F32)[None], (devices, image_count)),
        ],
        axis=1,
    )
    kept = jnp.broadcast_to(silu_low.astype(F32).reshape(1, -1), (devices, image_count * width))
    ready = jnp.concatenate([kept, ready], axis=1)
    if square:
        heads_blocks = z_sends(heads_rows)
        d_silu = ada_back(d_mod, w_ada, deps=(ready, mlp_z) + tuple(heads_blocks))
    else:
        d_silu = ada_back(d_mod, w_ada)
    d_cond = d_silu * cond_sig * (1.0 + cond_vec * (1.0 - cond_sig))
    message = jnp.concatenate(
        [jnp.broadcast_to(d_cond.reshape(1, -1), (devices, image_count * width)), ready], axis=1
    )
    if square:
        heads_z = reduce_z_steps(heads_blocks, d_cond)
        message, heads_z, mlp_z = lax.optimization_barrier((message, heads_z, mlp_z))
        swapped = swap_core(heads_z)
        grad_mlp = reduce_core(mlp_z)
        grad_gu, grad_down = grad_mlp[:, :, : 2 * units], grad_mlp[:, :, 2 * units :]
    arrived = lax.all_to_all(message, axes, 0, 0, tiled=True)
    table_rows = time_table.shape[0] // devices
    flat = (at_q * nc + at_c) * tn + at_z
    own_bins = flat * table_rows + jnp.arange(table_rows, dtype=jnp.int32)
    grad_ada, grad_b_ada, grad_bias, rms_values, grad_table = last_sums(
        arrived, own_bins[None, :].astype(F32), image_count, width, ada_cols, bias_cols
    )

    def joined(value, parts):
        both = [value[j].reshape(strip, parts, -1) for j in range(nc)]
        return jnp.concatenate(both, axis=2)

    grad_qkv, grad_out = place_heads(place, *swapped, hw)

    return (
        output,
        d_inputs,
        d_cond,
        grad_qkv.transpose(1, 0, 2),
        grad_out.T,
        joined(grad_gu, 2),
        joined(grad_down, 1)[:, 0].T,
        grad_ada.T,
        grad_b_ada[0],
        grad_bias[0],
        grad_table,
        rms_values[0],
    )


def solution(mesh):
    groups, tn = mesh.shape["dp"], mesh.shape["tensor"]
    nc, nx = 2, 2
    sizes = {"y": groups // (nx * nc), "x": nx, "c": nc, "z": tn}
    fine = Mesh(mesh.devices.reshape(tuple(sizes.values())), tuple(sizes))
    dp = ("y", "x", "c")
    every = dp + ("z",)
    return jax.shard_map(
        functools.partial(local, sizes),
        mesh=fine,
        in_specs=(
            P(every, None),
            P(every, None),
            P(every),
            P(every),
            P(None, every),
            P(),
            P(),
            P(),
            P(None, None, "z"),
            P("z", None),
            P(),
            P(None, None, "z"),
            P("z", None),
            P(every, None),
        ),
        out_specs=(
            P(every, None),
            P(every, None),
            P(every, None),
            P(dp, None, "z"),
            P("z", dp),
            P(dp, None, "z"),
            P("z", dp),
            P(None, every),
            P(every),
            P(every),
            P(every, None),
            P(),
        ),
        check_vma=False,
    )
```
